128 devices in a mesh: section: 8 (over z, core), dp: 16 (over y, x).
Axes of the slice: x: 4, y: 4, z: 4, core: 2. Of those that a mesh axis runs over, the one named last changes fastest.
Arguments:
- embedded: bfloat16 [2, 2048, 4096], P(None, 'dp'), may hold values from -6 to 6
- saved_inputs: bfloat16 [8, 2, 2048, 4096], P('section', None, 'dp'), may hold values from -6 to 6
- cotangent: bfloat16 [2, 2048, 4096], P(None, 'dp'), may hold values from -6 to 6
- w_down: bfloat16 [8, 512, 4096], P('section'), may hold values from -0.09375 to 0.09375
- w_up: bfloat16 [8, 512, 4096], P('section'), may hold values from -0.046875 to 0.046875
- bias: float32 [8, 4096], P('section'), may hold values from -3 to 3
- owners: int32 [2048, 2, 16, 1], P('dp'), may hold values from 0 to 127; in each aligned block of 512 rows (0 to 511, 512 to 1023, ..., all dimensions but the last counted through in order) at most 8 rows name the same one
- row_ids: int32 [2048, 2, 16], P('dp'), may hold values from 0 to 2047
Outputs:
- grad_down: float32 [8, 512, 4096], P('section', None, 'dp')
- grad_up: float32 [8, 512, 4096], P('section', None, 'dp')
- grad_bias: float32 [8, 4096], P('section', 'dp')
- table_grad: float32 [262144, 256], P(('section', 'dp'))
The draws below stay inside these ranges and needn't reach their ends.
Inputs may be any that keep to these rules, and one draw needn't show every extreme that they name: `owners`: in each aligned block of 512 lookups in the order (sample, micro-batch, feature) no owner is named more than 8 times, a bound that some block reaches.
All inputs are finite; a program needn't handle non-finite values.
Results may differ from the reference program's by a relative error of at most 0.015.
Values may be sent and summed in bfloat16 or wider, within the bound.
No kernel may reach another device: no remote copies, remote signals or barrier semaphores. Data moves between devices by JAX's collectives and lax.ppermute only.
A program may use at most 192 MiB of HBM per device.

```python
import math
import jax
import jax.numpy as jnp
import numpy as np

D = 4096
E = 256
R = 512
MB = 2
ROWS_DEV = 2048
F = 16
LAYERS = 8
BATCH = 2048
LOOK = 512
CAP = 8
N_SECTION = 8
N_DP = 16


def touch_ends(entries, stream_key, least, largest):
    longest = entries.shape.index(max(entries.shape))
    spots = []
    for shift in (0, 1):
        where = [jax.random.randint(jax.random.fold_in(stream_key, axis), (), 0, length) for axis, length in enumerate(entries.shape)]
        where[longest] = (where[longest] + shift) % entries.shape[longest]
        spots.append(tuple(where))
    return entries.at[spots[0]].set(least).at[spots[1]].set(largest)


def block_levels(key, extent, pieces, smallest, largest):
    gain, own = 1.0, jax.random.fold_in(key, 6)
    for position, parts in pieces:
        draws = jnp.exp(jax.random.uniform(jax.random.fold_in(own, position), (parts,), jnp.float32, smallest / len(pieces), largest / len(pieces)))
        gain = gain * jnp.repeat(draws, extent[position] // parts).reshape([-1 if axis == position else 1 for axis in range(len(extent))])
    return gain


def routed_block(own_key, own, number, rows, amount, top, bound, slope):
    sequence = jax.random.permutation(own_key, amount)
    crowded, usual = shares(amount, rows * top, bound, slope, True), shares(amount, rows * top, bound, slope, False)
    places = jnp.arange(amount)

    def named(lengths, rotation):
        used = int((lengths > 0).sum())
        fixed = max(1, used // 4)
        moved = fixed + (places - fixed + rotation * (used - fixed)) % max(1, amount - fixed)
        return jnp.zeros((amount,), jnp.int32).at[sequence[jnp.where(places < fixed, places, moved)]].set(jnp.asarray(lengths, jnp.int32))

    lengths = jnp.where(number % 4 == 0, named(crowded, number // 4), named(usual, number - number // 4 - 1))
    mixed = jax.random.permutation(jax.random.fold_in(own, 3), amount)
    source_of, taker = mixed[0:amount // 2 * 2:2], mixed[1:amount // 2 * 2:2]
    slack = jnp.minimum(lengths[source_of] - 1, bound - lengths[taker]) // 2
    slack = jnp.where((source_of == sequence[0]) | (taker == sequence[0]) | (lengths[taker] == 0), 0, jnp.maximum(slack, 0))
    moved = jax.random.randint(jax.random.fold_in(own, 4), (amount // 2,), 0, 1 << 20) % (slack + 1)
    lengths = lengths.at[source_of].add(-moved).at[taker].add(moved)
    items = jnp.searchsorted(jnp.cumsum(lengths), jnp.arange(rows * top), side="right").astype(jnp.int32)
    listing = items.reshape(top, rows).T
    listing = listing[jax.random.permutation(jax.random.fold_in(own, 1), rows)]
    rotation = jax.random.randint(jax.random.fold_in(own, 2), (rows, 1), 0, top)
    return jnp.take_along_axis(listing, (jnp.arange(top)[None, :] + rotation) % top, axis=1)


def shares(count, total, limit, slope, full):
    portions = [(1 << 20) // math.isqrt(grade ** slope) + 1 for grade in range(1, count + 1)]
    largest = limit if full else min(limit, max(-(-total // count), total * portions[0] // sum(portions)))
    least = 1 if total - largest >= count - 1 else 0
    counts, spare = [largest] + [least] * (count - 1), total - largest - least * (count - 1)
    while spare > 0:
        free = [i for i in range(1, count) if counts[i] < largest] or [i for i in range(1, count) if counts[i] < limit]
        mass, remaining = sum([portions[i] for i in free]), spare
        for i in free:
            addition = min(limit - counts[i], max(1, remaining * portions[i] // mass), spare)
            counts[i] = counts[i] + addition
            spare = spare - addition
    return np.array(counts)


def normal_values(rng, shape, spread, bound, cuts=(), dtype=jnp.bfloat16):
    array = spread * jax.random.normal(rng, shape, jnp.float32)
    if cuts:
        array = array * block_levels(rng, shape, cuts, -0.22, 0.18)
    return jnp.clip(array, -bound, bound).astype(dtype)


def setup_inputs(seed: int = 0) -> dict:
    splits = jax.random.split(jax.random.key(seed), 9)
    embedded = normal_values(splits[0], (MB, BATCH, D), 1.0, 6.0, ((1, 16),))
    saved_inputs = normal_values(splits[1], (LAYERS, MB, BATCH, D), 1.0, 6.0, ((0, 8), (2, 16)))
    cotangent = normal_values(splits[2], (MB, BATCH, D), 1.0, 6.0, ((1, 16),))
    w_down = normal_values(splits[3], (LAYERS, R, D), D ** -0.5, 0.09375, ((0, 8),))
    w_up = normal_values(splits[4], (LAYERS, R, D), (4 * D) ** -0.5, 0.046875, ((0, 8),))
    bias = normal_values(splits[5], (LAYERS, D), 0.5, 3.0, ((0, 8),), jnp.float32)
    owners_keys = jax.random.split(jax.random.fold_in(splits[6], 1), BATCH * MB * F // LOOK)
    owners_turns = jax.random.permutation(jax.random.fold_in(splits[6], 3), BATCH * MB * F // LOOK)
    owners = jax.vmap(lambda own, number: routed_block(jax.random.fold_in(splits[6], 2), own, number, LOOK, N_SECTION * N_DP, 1, CAP, 2))(owners_keys, owners_turns).reshape((BATCH, MB, F, 1))
    row_ids = touch_ends(jax.random.randint(splits[7], (BATCH, MB, F), 0, ROWS_DEV), jax.random.fold_in(splits[7], 1), 0, ROWS_DEV - 1).astype(jnp.int32)
    return {"embedded": embedded, "saved_inputs": saved_inputs, "cotangent": cotangent, "w_down": w_down, "w_up": w_up, "bias": bias, "owners": owners, "row_ids": row_ids}


def reference(embedded, saved_inputs, cotangent, w_down, w_up, bias, owners, row_ids):
    grad_down = jnp.zeros((LAYERS, R, D), jnp.float32)
    grad_up = jnp.zeros((LAYERS, R, D), jnp.float32)
    grad_bias = jnp.zeros((LAYERS, D), jnp.float32)
    input_grads = []
    for micro in range(MB):
        first = embedded[micro].astype(jnp.float32)
        incoming = cotangent[micro]
        total = jnp.zeros((BATCH, D), jnp.float32)
        for layer in range(LAYERS - 1, -1, -1):
            layer_in = saved_inputs[layer, micro]
            latent = jnp.dot(layer_in, w_down[layer].T, preferred_element_type=jnp.float32).astype(jnp.bfloat16)
            product = jnp.dot(latent, w_up[layer], preferred_element_type=jnp.float32) + bias[layer]
            upstream = incoming.astype(jnp.float32)
            grad_prod = upstream * first
            total = total + upstream * product
            grad_prod_b = grad_prod.astype(jnp.bfloat16)
            grad_up = grad_up.at[layer].add(jnp.dot(latent.T, grad_prod_b, preferred_element_type=jnp.float32))
            grad_bias = grad_bias.at[layer].add(jnp.sum(grad_prod, axis=0))
            grad_latent = jnp.dot(grad_prod_b, w_up[layer].T, preferred_element_type=jnp.float32).astype(jnp.bfloat16)
            grad_down = grad_down.at[layer].add(jnp.dot(grad_latent.T, layer_in, preferred_element_type=jnp.float32))
            passed = upstream + jnp.dot(grad_latent, w_down[layer], preferred_element_type=jnp.float32)
            if layer > 0:
                incoming = passed.astype(jnp.bfloat16)
            else:
                total = total + passed
        input_grads.append(total)
    stacked = jnp.stack(input_grads)
    row_grads = stacked.reshape(MB, BATCH, F, E).transpose(1, 0, 2, 3).reshape(-1, E)
    index = (owners[..., 0].reshape(-1) * ROWS_DEV + row_ids.reshape(-1)).astype(jnp.int32)
    table_grad = jax.ops.segment_sum(row_grads, index, num_segments=ROWS_DEV * N_SECTION * N_DP)
    return grad_down, grad_up, grad_bias, table_grad
```

```python
import jax
import jax.numpy as jnp
from jax import lax
from jax.sharding import PartitionSpec as P

E = 256
ROWS_DEV = 2048
CAP = 8
HALVES = 2
BF = jnp.bfloat16
F32 = jnp.float32


def dot(a, b, dims):
    return lax.dot_general(a, b, (dims, ((), ())), preferred_element_type=F32)


def exchange(pieces, axis):
    return lax.all_to_all(pieces, axis, split_axis=0, concat_axis=0, tiled=True)


def after(*arrays):
    return lax.optimization_barrier(arrays)


def in_columns(rows, devices):
    return rows.reshape(rows.shape[0], devices, -1).transpose(1, 0, 2)


def in_pieces(array, sections):
    micro, samples, width = array.shape
    share = samples // sections // HALVES
    array = array.reshape(micro, sections, HALVES, share, width).transpose(0, 2, 1, 3, 4)
    return array.reshape(micro * HALVES, sections * share, width)


def local(embedded, saved_inputs, cotangent, w_down, w_up, bias, owners, row_ids):
    sections = lax.axis_size("section")
    replicas = lax.axis_size("dp")
    section_id = lax.axis_index("section")
    devices = sections * replicas
    micro_count, samples, width = embedded.shape
    features = width // E
    rank = w_down.shape[1]
    pieces = micro_count * HALVES
    rows = samples // HALVES
    share = rows // sections
    sub = samples // sections
    turns = sections + pieces - 1
    down, up = w_down[0], w_up[0]

    emb = in_pieces(embedded, sections)
    cot = in_pieces(cotangent, sections)
    layer_in = in_pieces(saved_inputs[0], sections).reshape(-1, width)

    def block_of(array):
        array = lax.dynamic_slice_in_dim(array, section_id * sub, sub, 0)
        array = array.reshape(HALVES, share, micro_count, features)
        return array.transpose(3, 2, 0, 1).reshape(-1)

    own, ids = block_of(owners), block_of(row_ids)
    look = own.shape[0]
    order = jnp.arange(look, dtype=jnp.int32)
    earlier = (own[:, None] == own[None, :]) & (order[:, None] < order[None, :])
    slot = own * CAP + jnp.sum(earlier.astype(jnp.int32), axis=0)
    slots = devices * CAP
    put = jnp.arange(slots, dtype=jnp.int32)[:, None] == slot[None, :]
    send_rows = jnp.sum(jnp.where(put, ids[None, :], 0), axis=1)
    put = put.astype(BF)

    latent = dot(layer_in, down, ((1,), (1,))).astype(BF)
    product = (dot(latent, up, ((1,), (0,))) + bias[0]).reshape(pieces, rows, width)
    all_latent = lax.all_gather(latent, "dp", axis=0).reshape(replicas, pieces, rows, rank)

    got_g = jnp.zeros((pieces + 2, rows, width), BF)
    got_h = jnp.zeros((pieces + 2, rows, rank), BF)
    incoming = jnp.zeros((rows, width), BF)
    terms, all_gp = [], []
    for turn in range(turns):
        piece = turn - (sections - 1 - section_id)
        clipped = jnp.clip(piece, 0, pieces - 1)
        here = jnp.clip(piece, -1, pieces) + 1
        first = lax.dynamic_index_in_dim(emb, clipped, 0, keepdims=False)
        if turn == 2:
            incoming, got_rows = after(incoming, got_rows)
        if turn == 4:
            incoming, all_in = after(incoming, all_in)
        if turn == 6:
            incoming, product = after(incoming, product)
        if all_gp:
            incoming, all_gp[-1] = after(incoming, all_gp[-1])
        if turn < pieces:
            incoming = jnp.where(section_id == sections - 1, cot[turn], incoming)
        gp = (incoming.astype(F32) * first.astype(F32)).astype(BF)
        h = dot(gp, up, ((1,), (1,))).astype(BF)
        passed = (incoming.astype(F32) + dot(h, down, ((1,), (0,)))).astype(BF)
        if turn == 0:
            send_rows, _ = after(send_rows, passed)
            got_rows = exchange(send_rows.reshape(devices, CAP), ("section", "dp"))
        if turn == 1:
            columns, _, _ = after(in_columns(layer_in, replicas), passed, got_rows)
            all_in = exchange(columns, "dp")
        got_g = lax.dynamic_update_index_in_dim(got_g, incoming, here, 0)
        got_h = lax.dynamic_update_index_in_dim(got_h, h, here, 0)
        if turn < turns - 1:
            pairs = [(s, s - 1) for s in range(1, sections) if 0 <= turn - (sections - 1 - s) < pieces]
            incoming = lax.ppermute(passed, "section", pairs)
        k = turn - (sections - 1)
        if k >= 0:
            g = got_g[k + 1].astype(F32)
            last = jnp.where(section_id == 0, passed, jnp.zeros((), BF)).astype(F32)
            term = (g * product[k] + last).astype(BF)
            terms.append(term.reshape(sections, share, width))
            columns = in_columns((g * emb[k].astype(F32)).astype(BF), replicas)
            if k < pieces - 1:
                all_gp.append(exchange(columns, "dp"))
            if k == pieces - 2:
                early_h = lax.all_gather(got_h[1:pieces].reshape(-1, rank), "dp", axis=0)
                early = jnp.concatenate(terms, axis=1).reshape(-1, width)
                early = lax.psum_scatter(early, "section", scatter_dimension=0, tiled=True)
    end = exchange(terms[-1], "section")
    late = jnp.broadcast_to(got_h[pieces][None], (replicas, rows, rank))
    late = jnp.concatenate([columns, late], axis=2)
    late, end = after(late, end)
    late = exchange(late, "dp")
    all_gp.append(late[:, :, : width // replicas])
    late_h = late[:, :, width // replicas :]
    end = end.astype(F32).sum(axis=0).astype(BF)

    cut = (pieces - 1) * rows
    both = ((0, 1), (0, 1))
    grad_down = dot(early_h, all_in[:, :cut], both) + dot(late_h, all_in[:, cut:], both)
    grad_up = sum(dot(all_latent[:, k], all_gp[k], both) for k in range(pieces))
    grad_bias = sum(jnp.sum(gp.astype(F32), axis=(0, 1)) for gp in all_gp)

    row_grads = jnp.concatenate([early, end], axis=0)
    row_grads = in_columns(row_grads, features).reshape(-1, E)
    send = dot(put, row_grads, ((1,), (0,))).astype(BF).reshape(devices, CAP, E)
    send, late = after(send, late)
    got = exchange(send, ("section", "dp")).reshape(-1, E)
    ids_here = jnp.arange(ROWS_DEV, dtype=jnp.int32)
    table_put = (ids_here[:, None] == got_rows.reshape(1, -1)).astype(BF)
    table_grad = dot(table_put, got, ((1,), (0,)))
    return (grad_down[None], grad_up[None], grad_bias[None], table_grad)


def solution(mesh):
    placed = (
        P(None, "dp", None),
        P("section", None, "dp", None),
        P(None, "dp", None),
        P("section", None, None),
        P("section", None, None),
        P("section", None),
        P("dp", None, None, None),
        P("dp", None, None),
    )
    return jax.shard_map(
        local,
        mesh=mesh,
        in_specs=placed,
        out_specs=(
            P("section", None, "dp"),
            P("section", None, "dp"),
            P("section", "dp"),
            P(("section", "dp"), None),
        ),
        check_vma=False,
    )
```

```python
import jax
import jax.numpy as jnp
from jax import lax
from jax.experimental.layout import Layout, with_layout_constraint
from jax.sharding import PartitionSpec as P

E = 256
ROWS_DEV = 2048
CAP = 8
BF = jnp.bfloat16
F32 = jnp.float32


def dot(a, b, dims):
    return lax.dot_general(a, b, (dims, ((), ())), preferred_element_type=F32)


def exchange(pieces, axis):
    return lax.all_to_all(pieces, axis, split_axis=0, concat_axis=0, tiled=True)


def rows_major(array):
    return with_layout_constraint(array, Layout(major_to_minor=tuple(range(array.ndim))))


def after(*arrays):
    return lax.optimization_barrier(arrays)


def in_columns(rows, devices):
    return rows.reshape(rows.shape[0], devices, -1).transpose(1, 0, 2)


def local(embedded, saved_inputs, cotangent, w_down, w_up, bias, owners, row_ids):
    sections = lax.axis_size("section")
    replicas = lax.axis_size("dp")
    section_id = lax.axis_index("section")
    devices = sections * replicas
    pieces, rows, width = embedded.shape
    features = width // E
    rank = w_down.shape[1]
    share = rows // sections
    turns = sections + pieces - 1
    down, up = w_down[0], w_up[0]

    got_g, got_h = [None] * pieces, [None] * pieces
    incoming = jnp.zeros((rows, width), BF)
    layer_in = saved_inputs[0].reshape(-1, width)
    for turn in range(turns):
        piece = turn - (sections - 1 - section_id)
        clipped = jnp.clip(piece, 0, pieces - 1)
        first = lax.dynamic_index_in_dim(embedded, clipped, 0, keepdims=False)
        if turn == 2:
            incoming, latent = after(incoming, latent)
        if turn == 4:
            incoming, product = after(incoming, product)
        if turn == 6:
            incoming, all_in, put, send_ids = after(incoming, all_in, put, send_ids)
        if turn == 7:
            incoming, all_latent = after(incoming, all_latent)
        if turn == sections:
            incoming, all_gp[0] = after(incoming, all_gp[0])
        if turn < pieces:
            incoming = jnp.where(section_id == sections - 1, cotangent[turn], incoming)
        gp = (incoming.astype(F32) * first.astype(F32)).astype(BF)
        h = dot(gp, up, ((1,), (1,))).astype(BF)
        passed = (incoming.astype(F32) + dot(h, down, ((1,), (0,)))).astype(BF)
        if turn < turns - 1:
            pairs = [(s, s - 1) for s in range(1, sections) if 0 <= turn - (sections - 1 - s) < pieces]
            arriving = lax.ppermute(passed, "section", pairs)
        for k in range(pieces):
            if turn == k:
                got_g[k], got_h[k] = incoming, h
            elif 0 <= turn - k < sections:
                old_g, old_h, _ = after(got_g[k], got_h[k], passed)
                got_g[k] = jnp.where(piece == k, incoming, old_g)
                got_h[k] = jnp.where(piece == k, h, old_h)

        if turn == 1:
            there = rows_major(after(layer_in, passed)[0])
            latent = dot(there, down, ((1,), (1,))).astype(BF)
            all_in = rows_major(exchange(rows_major(in_columns(there, replicas)), "dp"))
        if turn == 3:
            latent, _ = after(latent, passed)
            product = (dot(latent, up, ((1,), (0,))) + bias[0]).reshape(pieces, rows, width)
            all_latent = lax.all_gather(latent, "dp", axis=0).reshape(replicas, pieces, rows, rank)
        if turn == 5:
            own, ids, _ = after(owners, row_ids, passed)
            own = lax.dynamic_slice_in_dim(own, section_id * share, share, 0).transpose(2, 1, 0, 3).reshape(-1)
            ids = lax.dynamic_slice_in_dim(ids, section_id * share, share, 0).transpose(2, 1, 0).reshape(-1)
            order = jnp.arange(own.shape[0], dtype=jnp.int32)
            earlier = (own[:, None] == own[None, :]) & (order[:, None] < order[None, :])
            slot = own * CAP + jnp.sum(earlier.astype(jnp.int32), axis=0)
            put = jnp.arange(devices * CAP, dtype=jnp.int32)[:, None] == slot[None, :]
            send_ids = jnp.sum(jnp.where(put, ids[None, :], 0), axis=1)
            put = put.astype(BF)
        k = turn - (sections - 1)
        if k >= 0:
            g = got_g[k].astype(F32)
            last = jnp.where(section_id == 0, passed, jnp.zeros((), BF)).astype(F32)
            term = (g * product[k] + last).astype(BF)
            columns = in_columns((g * embedded[k].astype(F32)).astype(BF), replicas)
        if k == 0:
            summed = [lax.psum_scatter(term, "section", scatter_dimension=0, tiled=True)]
            all_h = [lax.all_gather(got_h[0], "dp", axis=0)]
            all_gp = [exchange(columns, "dp")]
        if turn < turns - 1:
            incoming = arriving
    term, all_gp[0] = after(term, all_gp[0])
    terms = exchange(term.reshape(sections, share, width), "section")
    all_h.append(lax.all_gather(got_h[1], "dp", axis=0))
    columns, terms, summed[0], all_h[0] = after(columns, terms, summed[0], all_h[0])
    all_gp.append(exchange(columns, "dp"))
    summed.append(terms.astype(F32).sum(axis=0).astype(BF))

    row_grads = in_columns(jnp.concatenate(summed, axis=0), features).reshape(-1, E)
    send = rows_major(dot(put, row_grads, ((1,), (0,))).astype(BF))
    high, low = send_ids // 256, send_ids % 256
    ids = jnp.stack([high, low], axis=1).astype(BF)
    ids = rows_major(jnp.pad(ids, ((0, 0), (0, 126))))
    send = jnp.concatenate([send, ids], axis=1).reshape(devices, CAP, -1)
    send, all_gp[1] = after(send, all_gp[1])
    got = exchange(send, ("section", "dp")).reshape(devices * CAP, -1)

    both = ((0, 1), (0, 1))
    all_in = all_in.reshape(replicas, pieces, rows, -1)
    grad_down = sum(dot(all_h[k], all_in[:, k], both) for k in range(pieces))
    grad_up = sum(dot(all_latent[:, k], all_gp[k], both) for k in range(pieces))
    grad_bias = sum(jnp.sum(gp.astype(F32), axis=(0, 1)) for gp in all_gp)

    got_ids = (got[:, E].astype(F32) * 256 + got[:, E + 1].astype(F32)).astype(jnp.int32)
    table_put = (jnp.arange(ROWS_DEV, dtype=jnp.int32)[:, None] == got_ids[None, :]).astype(BF)
    table_grad = dot(table_put, got[:, :E], ((1,), (0,)))
    return (grad_down[None], grad_up[None], grad_bias[None], table_grad)


def solution(mesh):
    placed = (
        P(None, "dp", None),
        P("section", None, "dp", None),
        P(None, "dp", None),
        P("section", None, None),
        P("section", None, None),
        P("section", None),
        P("dp", None, None, None),
        P("dp", None, None),
    )
    return jax.shard_map(
        local,
        mesh=mesh,
        in_specs=placed,
        out_specs=(
            P("section", None, "dp"),
            P("section", None, "dp"),
            P("section", "dp"),
            P(("section", "dp"), None),
        ),
        check_vma=False,
    )
```

```python
import math

import jax
import jax.numpy as jnp
from jax import lax
from jax.experimental.layout import Layout, with_layout_constraint
from jax.sharding import PartitionSpec as P

E = 256
ROWS_DEV = 2048
CAP = 8
BF = jnp.bfloat16
F32 = jnp.float32


def dot(a, b, dims):
    return lax.dot_general(a, b, (dims, ((), ())), preferred_element_type=F32)


def exchange(pieces, axis):
    return lax.all_to_all(pieces, axis, split_axis=0, concat_axis=0, tiled=True)


def rows_major(array):
    return with_layout_constraint(array, Layout(major_to_minor=tuple(range(array.ndim))))


def after(*arrays):
    return lax.optimization_barrier(arrays)


def in_columns(rows, devices):
    return rows.reshape(rows.shape[0], devices, -1).transpose(1, 0, 2)


def ring(sizes, place, shift):
    pairs = []
    stride = 1
    for size in sizes[place + 1 :]:
        stride *= size
    count = 1
    for size in sizes:
        count *= size
    for i in range(count):
        here = i // stride % sizes[place]
        pairs.append((i, i + ((here + shift) % sizes[place] - here) * stride))
    return pairs


def sum_over_section(term, sections, section_id):
    chips = sections // 2
    chip, core = section_id // 2, section_id % 2
    term = term.reshape(chips, 2, -1, term.shape[1])
    other = lax.dynamic_index_in_dim(term, 1 - core, 1, keepdims=False)
    mine = lax.dynamic_index_in_dim(term, core, 1, keepdims=False)
    other = lax.ppermute(other, "section", ring((chips, 2), 1, 1))
    both = (mine.astype(F32) + other.astype(F32)).astype(BF)
    total = lax.dynamic_index_in_dim(both, chip, 0, keepdims=False).astype(F32)
    for d in range(1, chips):
        block = lax.dynamic_index_in_dim(both, (chip + d) % chips, 0, keepdims=False)
        total = total + lax.ppermute(block, "section", ring((chips, 2), 0, d)).astype(F32)
    return total.astype(BF)


def gather_line(block, side, place):
    return [block] + [lax.ppermute(block, "dp", ring((side, side), place, d)) for d in range(1, side)]


def local(embedded, saved_inputs, cotangent, w_down, w_up, bias, owners, row_ids):
    sections = lax.axis_size("section")
    replicas = lax.axis_size("dp")
    section_id = lax.axis_index("section")
    dp_id = lax.axis_index("dp")
    side = math.isqrt(replicas)
    dp_y, dp_x = dp_id // side, dp_id % side
    devices = sections * replicas
    pieces, rows, width = embedded.shape
    features = width // E
    rank = w_down.shape[1]
    share = rows // sections
    turns = sections + pieces - 1
    down, up = w_down[0], w_up[0]

    held_g, held_h = [None] * pieces, [None] * pieces
    odd = (sections - 1 - section_id) % 2 == 1
    incoming = jnp.zeros((rows, width), BF)
    layer_in = saved_inputs[0].reshape(-1, width)

    def piece_of(held, k):
        return jnp.where(odd, held[1 - k], held[k])

    def terms_of(k, passed):
        g = piece_of(held_g, k).astype(F32)
        last = jnp.where(section_id == 0, passed, jnp.zeros((), BF)).astype(F32)
        term = (g * product[k] + last).astype(BF)
        return term, in_columns((g * embedded[k].astype(F32)).astype(BF), replicas)

    for turn in range(turns):
        piece = turn - (sections - 1 - section_id)
        valid = (piece >= 0) & (piece < pieces)
        clipped = jnp.clip(piece, 0, pieces - 1)
        first = lax.dynamic_index_in_dim(embedded, clipped, 0, keepdims=False)
        if turn == 2:
            incoming, latent = after(incoming, latent)
        if turn == 4:
            incoming, product = after(incoming, product)
        if turn == 6:
            incoming, all_in, put, send_ids = after(incoming, all_in, put, send_ids)
        if turn == sections:
            incoming, all_gp, summed = after(incoming, all_gp, summed)
        if turn < pieces:
            incoming = jnp.where(section_id == sections - 1, cotangent[turn], incoming)
        gp = (incoming.astype(F32) * first.astype(F32)).astype(BF)
        h = dot(gp, up, ((1,), (1,))).astype(BF)
        passed = (incoming.astype(F32) + dot(h, down, ((1,), (0,)))).astype(BF)
        if turn < turns - 1:
            pairs = [(s, s - 1) for s in range(1, sections) if 0 <= turn - (sections - 1 - s) < pieces]
            arriving = lax.ppermute(passed, "section", pairs)
        slot = turn % pieces
        if turn < pieces:
            held_g[slot], held_h[slot] = incoming, h
        else:
            old_g, old_h, _ = after(held_g[slot], held_h[slot], passed)
            held_g[slot] = jnp.where(valid, incoming, old_g)
            held_h[slot] = jnp.where(valid, h, old_h)

        if turn == 1:
            there = rows_major(after(layer_in, passed)[0])
            latent = dot(there, down, ((1,), (1,))).astype(BF)
            all_in = rows_major(exchange(rows_major(in_columns(there, replicas)), "dp"))
        if turn == 3:
            latent, _ = after(latent, passed)
            product = (dot(latent, up, ((1,), (0,))) + bias[0]).reshape(pieces, rows, width)
            all_latent = lax.all_gather(latent, "dp", axis=0).reshape(replicas, pieces, rows, rank)
        if turn == 5:
            own, ids, _ = after(owners, row_ids, passed)
            own = lax.dynamic_slice_in_dim(own, section_id * share, share, 0).transpose(2, 1, 0, 3).reshape(-1)
            ids = lax.dynamic_slice_in_dim(ids, section_id * share, share, 0).transpose(2, 1, 0).reshape(-1)
            order = jnp.arange(own.shape[0], dtype=jnp.int32)
            earlier = (own[:, None] == own[None, :]) & (order[:, None] < order[None, :])
            place = own * CAP + jnp.sum(earlier.astype(jnp.int32), axis=0)
            put = jnp.arange(devices * CAP, dtype=jnp.int32)[:, None] == place[None, :]
            send_ids = jnp.sum(jnp.where(put, ids[None, :], 0), axis=1)
            put = put.astype(BF)
        if turn == sections - 1:
            first_h = lax.all_gather(piece_of(held_h, 0), "dp", axis=0)
            term, columns = terms_of(0, passed)
            all_gp = exchange(columns, "dp")
            summed = sum_over_section(term, sections, section_id)
        if turn < turns - 1:
            incoming = arriving
    term, columns = terms_of(1, passed)
    all_gp = [all_gp, exchange(columns, "dp")]
    summed = [summed, sum_over_section(term, sections, section_id)]
    line = gather_line(piece_of(held_h, 1), side, 1)
    line = jnp.stack(line)
    plane = gather_line(line, side, 0)

    row_grads = in_columns(jnp.concatenate(summed, axis=0), features).reshape(-1, E)
    send = rows_major(dot(put, row_grads, ((1,), (0,))).astype(BF))
    high, low = send_ids // 256, send_ids % 256
    ids = jnp.stack([high, low], axis=1).astype(BF)
    ids = rows_major(jnp.pad(ids, ((0, 0), (0, 126))))
    send = jnp.concatenate([send, ids], axis=1).reshape(devices, CAP, -1)
    send, all_gp[1], all_latent = after(send, all_gp[1], all_latent)
    got = rows_major(exchange(send, ("section", "dp")).reshape(devices * CAP, -1))
    got, first_h = after(got, first_h)
    got = rows_major(got)

    both = ((0, 1), (0, 1))
    all_in = all_in.reshape(replicas, pieces, rows, -1)
    second_in = all_in[:, 1].reshape(side, side, rows, -1)
    second_in = jnp.stack([lax.dynamic_index_in_dim(second_in, (dp_x - d) % side, 1, keepdims=False) for d in range(side)], axis=1)
    grad_down = dot(first_h, all_in[:, 0], both)
    for d in range(side):
        grad_down = grad_down + dot(plane[d], lax.dynamic_index_in_dim(second_in, (dp_y - d) % side, 0, keepdims=False), both)
    grad_up = sum(dot(all_latent[:, k], all_gp[k], both) for k in range(pieces))
    grad_bias = sum(jnp.sum(gp.astype(F32), axis=(0, 1)) for gp in all_gp)

    got_ids = (got[:, E].astype(F32) * 256 + got[:, E + 1].astype(F32)).astype(jnp.int32)
    table_put = (jnp.arange(ROWS_DEV, dtype=jnp.int32)[:, None] == got_ids[None, :]).astype(BF)
    table_grad = dot(table_put, got[:, :E], ((1,), (0,)))
    return (grad_down[None], grad_up[None], grad_bias[None], table_grad)


def solution(mesh):
    placed = (
        P(None, "dp", None),
        P("section", None, "dp", None),
        P(None, "dp", None),
        P("section", None, None),
        P("section", None, None),
        P("section", None),
        P("dp", None, None, None),
        P("dp", None, None),
    )
    return jax.shard_map(
        local,
        mesh=mesh,
        in_specs=placed,
        out_specs=(
            P("section", None, "dp"),
            P("section", None, "dp"),
            P("section", "dp"),
            P(("section", "dp"), None),
        ),
        check_vma=False,
    )
```

```python
import math

import jax
import jax.numpy as jnp
from jax import lax
from jax.experimental.layout import Layout, with_layout_constraint
from jax.sharding import PartitionSpec as P

E = 256
ROWS_DEV = 2048
CAP = 8
BF = jnp.bfloat16
F32 = jnp.float32


def dot(a, b, dims):
    return lax.dot_general(a, b, (dims, ((), ())), preferred_element_type=F32)


def exchange(pieces, axis):
    return lax.all_to_all(pieces, axis, split_axis=0, concat_axis=0, tiled=True)


def rows_major(array):
    return with_layout_constraint(array, Layout(major_to_minor=tuple(range(array.ndim))))


def after(*arrays):
    return lax.optimization_barrier(arrays)


def in_columns(rows, devices):
    return rows.reshape(rows.shape[0], devices, -1).transpose(1, 0, 2)


def ring(sizes, place, shift):
    pairs = []
    stride = 1
    for size in sizes[place + 1 :]:
        stride *= size
    count = 1
    for size in sizes:
        count *= size
    for i in range(count):
        here = i // stride % sizes[place]
        pairs.append((i, i + ((here + shift) % sizes[place] - here) * stride))
    return pairs


def sum_over_section(terms, sections, section_id):
    chips = sections // 2
    chip, core = section_id // 2, section_id % 2
    pieces, rows, width = terms.shape
    terms = terms.reshape(pieces, chips, 2, rows // sections, width)
    other = lax.dynamic_index_in_dim(terms, 1 - core, 2, keepdims=False)
    mine = lax.dynamic_index_in_dim(terms, core, 2, keepdims=False)
    other = lax.ppermute(other, "section", ring((chips, 2), 1, 1))
    both = (mine.astype(F32) + other.astype(F32)).astype(BF)
    total = lax.dynamic_index_in_dim(both, chip, 1, keepdims=False).astype(F32)
    for d in range(1, chips):
        block = lax.dynamic_index_in_dim(both, (chip + d) % chips, 1, keepdims=False)
        total = total + lax.ppermute(block, "section", ring((chips, 2), 0, d)).astype(F32)
    return total.astype(BF).reshape(-1, width)


def gather_line(block, side, place):
    return [block] + [lax.ppermute(block, "dp", ring((side, side), place, d)) for d in range(1, side)]


def local(embedded, saved_inputs, cotangent, w_down, w_up, bias, owners, row_ids):
    sections = lax.axis_size("section")
    replicas = lax.axis_size("dp")
    section_id = lax.axis_index("section")
    dp_id = lax.axis_index("dp")
    side = math.isqrt(replicas)
    dp_y, dp_x = dp_id // side, dp_id % side
    devices = sections * replicas
    pieces, rows, width = embedded.shape
    features = width // E
    rank = w_down.shape[1]
    share = rows // sections
    turns = sections + pieces - 1
    down, up = w_down[0], w_up[0]

    held_g, held_h = [None] * pieces, [None] * pieces
    odd = (sections - 1 - section_id) % 2 == 1
    incoming = jnp.zeros((rows, width), BF)
    layer_in = saved_inputs[0].reshape(-1, width)

    def piece_of(held, k):
        return jnp.where(odd, held[1 - k], held[k])

    def terms_of(k, passed):
        g = piece_of(held_g, k).astype(F32)
        last = jnp.where(section_id == 0, passed, jnp.zeros((), BF)).astype(F32)
        term = (g * product[k] + last).astype(BF)
        return term, in_columns((g * embedded[k].astype(F32)).astype(BF), replicas)

    for turn in range(turns):
        piece = turn - (sections - 1 - section_id)
        valid = (piece >= 0) & (piece < pieces)
        clipped = jnp.clip(piece, 0, pieces - 1)
        first = lax.dynamic_index_in_dim(embedded, clipped, 0, keepdims=False)
        if turn == 2:
            incoming, latent = after(incoming, latent)
        if turn == 4:
            incoming, product = after(incoming, product)
        if turn == 6:
            incoming, all_in, put, ids = after(incoming, all_in, put, ids)
        if turn == 7:
            incoming, second_in = after(incoming, second_in)
        if turn == sections:
            incoming, all_gp = after(incoming, all_gp)
        if turn < pieces:
            incoming = jnp.where(section_id == sections - 1, cotangent[turn], incoming)
        gp = (incoming.astype(F32) * first.astype(F32)).astype(BF)
        h = dot(gp, up, ((1,), (1,))).astype(BF)
        passed = (incoming.astype(F32) + dot(h, down, ((1,), (0,)))).astype(BF)
        if turn < turns - 1:
            pairs = [(s, s - 1) for s in range(1, sections) if 0 <= turn - (sections - 1 - s) < pieces]
            arriving = lax.ppermute(passed, "section", pairs)
        slot = turn % pieces
        if turn < pieces:
            held_g[slot], held_h[slot] = incoming, h
        else:
            old_g, old_h, _ = after(held_g[slot], held_h[slot], passed)
            held_g[slot] = jnp.where(valid, incoming, old_g)
            held_h[slot] = jnp.where(valid, h, old_h)

        if turn == 1:
            there = rows_major(after(layer_in, passed)[0])
            latent = dot(there, down, ((1,), (1,))).astype(BF)
            all_in = rows_major(exchange(rows_major(in_columns(there, replicas)), "dp"))
        if turn == 3:
            latent, _ = after(latent, passed)
            product = (dot(latent, up, ((1,), (0,))) + bias[0]).reshape(pieces, rows, width)
            all_latent = lax.all_gather(latent, "dp", axis=0).reshape(replicas, pieces, rows, rank)
        if turn == 5:
            own, ids, _ = after(owners, row_ids, passed)
            own = lax.dynamic_slice_in_dim(own, section_id * share, share, 0).transpose(2, 1, 0, 3).reshape(-1)
            ids = lax.dynamic_slice_in_dim(ids, section_id * share, share, 0).transpose(2, 1, 0).reshape(-1)
            order = jnp.arange(own.shape[0], dtype=jnp.int32)
            earlier = (own[:, None] == own[None, :]) & (order[:, None] < order[None, :])
            place = own * CAP + jnp.sum(earlier.astype(jnp.int32), axis=0)
            put = jnp.arange(devices * CAP, dtype=jnp.int32)[:, None] == place[None, :]
            send_ids = jnp.sum(jnp.where(put, ids[None, :], 0), axis=1)
            put = put.astype(BF)
            ids = jnp.stack([send_ids // 256, send_ids % 256], axis=1).astype(BF)
            ids = rows_major(jnp.pad(ids, ((0, 0), (0, 126))))
        if turn == 6:
            all_in, _ = after(all_in, passed)
            all_in = all_in.reshape(replicas, pieces, rows, -1)
            second_in = all_in[:, 1].reshape(side, side, rows, -1)
            second_in = jnp.concatenate([lax.dynamic_index_in_dim(second_in, (dp_x - d) % side, 1) for d in range(side)], axis=1)
            second_in = jnp.concatenate([lax.dynamic_index_in_dim(second_in, (dp_y - d) % side, 0) for d in range(side)])
        if turn == sections - 1:
            first_h = lax.all_gather(piece_of(held_h, 0), "dp", axis=0)
            term, columns = terms_of(0, passed)
            terms = [term]
            all_gp = exchange(columns, "dp")
        if turn < turns - 1:
            incoming = arriving
    term, columns = terms_of(1, passed)
    summed = sum_over_section(jnp.stack([*terms, term]), sections, section_id)
    all_gp = [all_gp, exchange(columns, "dp")]
    line = gather_line(piece_of(held_h, 1), side, 1)
    line = jnp.stack(line)
    plane = gather_line(line, side, 0)

    row_grads = in_columns(summed, features).reshape(-1, E)
    send = rows_major(dot(put, row_grads, ((1,), (0,))).astype(BF))
    send = jnp.concatenate([send, ids], axis=1).reshape(devices, CAP, -1)
    send, all_gp[1], all_latent = after(send, all_gp[1], all_latent)
    got = rows_major(exchange(send, ("section", "dp")).reshape(devices * CAP, -1))
    got, first_h, *plane = after(got, first_h, *plane)
    got = rows_major(got)

    both = ((0, 1), (0, 1))
    grad_down = dot(first_h, all_in[:, 0], both) + dot(jnp.stack(plane), second_in, ((0, 1, 2), (0, 1, 2)))
    grad_up = sum(dot(all_latent[:, k], all_gp[k], both) for k in range(pieces))
    grad_bias = sum(jnp.sum(gp.astype(F32), axis=(0, 1)) for gp in all_gp)

    got_ids = (got[:, E].astype(F32) * 256 + got[:, E + 1].astype(F32)).astype(jnp.int32)
    table_put = (jnp.arange(ROWS_DEV, dtype=jnp.int32)[:, None] == got_ids[None, :]).astype(BF)
    table_grad = dot(table_put, got[:, :E], ((1,), (0,)))
    return (grad_down[None], grad_up[None], grad_bias[None], table_grad)


def solution(mesh):
    placed = (
        P(None, "dp", None),
        P("section", None, "dp", None),
        P(None, "dp", None),
        P("section", None, None),
        P("section", None, None),
        P("section", None),
        P("dp", None, None, None),
        P("dp", None, None),
    )
    return jax.shard_map(
        local,
        mesh=mesh,
        in_specs=placed,
        out_specs=(
            P("section", None, "dp"),
            P("section", None, "dp"),
            P("section", "dp"),
            P(("section", "dp"), None),
        ),
        check_vma=False,
    )
```

```python
import jax
import jax.numpy as jnp
from jax import lax
from jax.experimental.layout import Layout, with_layout_constraint
from jax.sharding import PartitionSpec as P

E = 256
ROWS_DEV = 2048
CAP = 8
BF = jnp.bfloat16
F32 = jnp.float32


def dot(a, b, dims):
    return lax.dot_general(a, b, (dims, ((), ())), preferred_element_type=F32)


def exchange(pieces, axis):
    return lax.all_to_all(pieces, axis, split_axis=0, concat_axis=0, tiled=True)


def rows_major(array):
    return with_layout_constraint(array, Layout(major_to_minor=tuple(range(array.ndim))))


def after(*arrays):
    return lax.optimization_barrier(arrays)


def in_columns(rows, devices):
    return rows.reshape(rows.shape[0], devices, -1).transpose(1, 0, 2)


def ring(sizes, place, shift):
    pairs = []
    stride = 1
    for size in sizes[place + 1 :]:
        stride *= size
    count = 1
    for size in sizes:
        count *= size
    for i in range(count):
        here = i // stride % sizes[place]
        pairs.append((i, i + ((here + shift) % sizes[place] - here) * stride))
    return pairs


def sum_over_section(terms, sections, section_id):
    chips = sections // 2
    chip, core = section_id // 2, section_id % 2
    pieces, rows, width = terms.shape
    terms = terms.reshape(pieces, chips, 2, rows // sections, width)
    other = lax.dynamic_index_in_dim(terms, 1 - core, 2, keepdims=False)
    mine = lax.dynamic_index_in_dim(terms, core, 2, keepdims=False)
    other = lax.ppermute(other, "section", ring((chips, 2), 1, 1))
    both = (mine.astype(F32) + other.astype(F32)).astype(BF)
    total = lax.dynamic_index_in_dim(both, chip, 1, keepdims=False).astype(F32)
    for d in range(1, chips):
        block = lax.dynamic_index_in_dim(both, (chip + d) % chips, 1, keepdims=False)
        total = total + lax.ppermute(block, "section", ring((chips, 2), 0, d)).astype(F32)
    return total.astype(BF).reshape(-1, width)


def local(embedded, saved_inputs, cotangent, w_down, w_up, bias, owners, row_ids):
    sections = lax.axis_size("section")
    replicas = lax.axis_size("dp")
    section_id = lax.axis_index("section")
    devices = sections * replicas
    pieces, rows, width = embedded.shape
    features = width // E
    rank = w_down.shape[1]
    share = rows // sections
    turns = sections + pieces - 1
    down, up = w_down[0], w_up[0]

    held_g, held_h = [None] * pieces, [None] * pieces
    odd = (sections - 1 - section_id) % 2 == 1
    incoming = jnp.zeros((rows, width), BF)
    layer_in = saved_inputs[0].reshape(-1, width)

    def piece_of(held, k):
        return jnp.where(odd, held[1 - k], held[k])

    def terms_of(k, passed):
        g = piece_of(held_g, k).astype(F32)
        bottom = jnp.where(section_id == 0, passed, jnp.zeros((), BF)).astype(F32)
        term = (g * product[k] + bottom).astype(BF)
        return term, in_columns((g * embedded[k].astype(F32)).astype(BF), replicas)

    last = []
    for turn in range(turns):
        piece = turn - (sections - 1 - section_id)
        valid = (piece >= 0) & (piece < pieces)
        clipped = jnp.clip(piece, 0, pieces - 1)
        first = lax.dynamic_index_in_dim(embedded, clipped, 0, keepdims=False)
        if turn == 2:
            incoming, latent = after(incoming, latent)
        if turn == 4:
            incoming, product = after(incoming, product)
        if turn == 6:
            incoming, all_in, put, ids = after(incoming, all_in, put, ids)
        if turn < pieces:
            incoming = jnp.where(section_id == sections - 1, cotangent[turn], incoming)
        gp = (incoming.astype(F32) * first.astype(F32)).astype(BF)
        h = dot(gp, up, ((1,), (1,))).astype(BF)
        passed = (incoming.astype(F32) + dot(h, down, ((1,), (0,)))).astype(BF)
        if turn < turns - 1:
            pairs = [(s, s - 1) for s in range(1, sections) if 0 <= turn - (sections - 1 - s) < pieces]
            arriving = lax.ppermute(passed, "section", pairs)
        slot = turn % pieces
        if turn < pieces:
            held_g[slot], held_h[slot] = incoming, h
        else:
            old_g, old_h, _ = after(held_g[slot], held_h[slot], passed)
            held_g[slot] = jnp.where(valid, incoming, old_g)
            held_h[slot] = jnp.where(valid, h, old_h)

        if turn == 1:
            there = rows_major(after(layer_in, passed)[0])
            latent = dot(there, down, ((1,), (1,))).astype(BF)
            all_in = rows_major(exchange(rows_major(in_columns(there, replicas)), "dp"))
        if turn == 3:
            latent, _ = after(latent, passed)
            product = (dot(latent, up, ((1,), (0,))) + bias[0]).reshape(pieces, rows, width)
            all_latent = lax.all_gather(latent, "dp", axis=0)
        if turn == 5:
            own, ids, _ = after(owners, row_ids, passed)
            own = lax.dynamic_slice_in_dim(own, section_id * share, share, 0).transpose(2, 1, 0, 3).reshape(-1)
            ids = lax.dynamic_slice_in_dim(ids, section_id * share, share, 0).transpose(2, 1, 0).reshape(-1)
            order = jnp.arange(own.shape[0], dtype=jnp.int32)
            earlier = (own[:, None] == own[None, :]) & (order[:, None] < order[None, :])
            place = own * CAP + jnp.sum(earlier.astype(jnp.int32), axis=0)
            put = jnp.arange(devices * CAP, dtype=jnp.int32)[:, None] == place[None, :]
            send_ids = jnp.sum(jnp.where(put, ids[None, :], 0), axis=1)
            put = put.astype(BF)
            ids = jnp.stack([send_ids // 256, send_ids % 256], axis=1).astype(BF)
            ids = rows_major(jnp.pad(ids, ((0, 0), (0, 126))))
        last.append(passed)
        if turn < turns - 1:
            incoming = arriving
    last = last[-pieces:]
    terms, columns = zip(*(terms_of(k, last[k]) for k in range(pieces)))
    all_h = lax.all_gather(jnp.stack([piece_of(held_h, k) for k in range(pieces)]), "dp", axis=0)
    summed = sum_over_section(jnp.stack(terms), sections, section_id)
    all_gp = exchange(jnp.concatenate(columns, axis=1), "dp")

    row_grads = in_columns(summed, features).reshape(-1, E)
    send = rows_major(dot(put, row_grads, ((1,), (0,))).astype(BF))
    send = jnp.concatenate([send, ids], axis=1).reshape(devices, CAP, -1)
    send, all_gp, all_latent = after(send, all_gp, all_latent)
    got = exchange(send, ("section", "dp")).reshape(devices * CAP, -1)
    got, all_h = after(got, all_h)
    got = rows_major(got)

    all_in = all_in.reshape(replicas, pieces, rows, -1)
    grad_down = dot(all_h, all_in, ((0, 1, 2), (0, 1, 2)))
    grad_up = dot(all_latent, all_gp, ((0, 1), (0, 1)))
    grad_bias = jnp.sum(all_gp.astype(F32), axis=(0, 1))

    got_ids = (got[:, E].astype(F32) * 256 + got[:, E + 1].astype(F32)).astype(jnp.int32)
    table_put = (jnp.arange(ROWS_DEV, dtype=jnp.int32)[:, None] == got_ids[None, :]).astype(BF)
    table_grad = dot(table_put, got[:, :E], ((1,), (0,)))
    return (grad_down[None], grad_up[None], grad_bias[None], table_grad)


def solution(mesh):
    placed = (
        P(None, "dp", None),
        P("section", None, "dp", None),
        P(None, "dp", None),
        P("section", None, None),
        P("section", None, None),
        P("section", None),
        P("dp", None, None, None),
        P("dp", None, None),
    )
    return jax.shard_map(
        local,
        mesh=mesh,
        in_specs=placed,
        out_specs=(
            P("section", None, "dp"),
            P("section", None, "dp"),
            P("section", "dp"),
            P(("section", "dp"), None),
        ),
        check_vma=False,
    )
```

```python
import functools

import jax
import jax.numpy as jnp
from jax import lax
from jax.experimental import pallas as pl
from jax.experimental.pallas import tpu as pltpu
from jax.experimental.layout import Layout, with_layout_constraint
from jax.sharding import PartitionSpec as P

E = 256
ROWS_DEV = 2048
CAP = 8
BF = jnp.bfloat16
F32 = jnp.float32


def dot(a, b, dims):
    return lax.dot_general(a, b, (dims, ((), ())), preferred_element_type=F32)


def exchange(pieces, axis):
    return lax.all_to_all(pieces, axis, split_axis=0, concat_axis=0, tiled=True)


def rows_major(array):
    return with_layout_constraint(array, Layout(major_to_minor=tuple(range(array.ndim))))


def after(*arrays):
    return lax.optimization_barrier(arrays)


def in_columns(rows, devices):
    return rows.reshape(rows.shape[0], devices, -1).transpose(1, 0, 2)


def turn_kernel(chunks, has_other, which, *refs):
    sources = list(refs[: 4 + has_other])
    passed, h_out = refs[4 + has_other : 6 + has_other]
    g, e, up, down, other, out, h, acc, sems, out_sems = refs[6 + has_other :]
    wide = g.shape[1] // chunks
    g_in, e_in, up_in, down_in = sources[:4]

    def part(k):
        return pl.ds(k * wide, wide)

    def bring(source, target, kind, k):
        return pltpu.make_async_copy(source.at[:, part(k)], target.at[:, part(k)], sems.at[kind, k])

    def bring_in(k):
        copies = [bring(g_in, g, 0, k), bring(e_in.at[which[0]], e, 1, k), bring(up_in, up, 2, k)]
        if has_other:
            copies.append(bring(sources[4], other, 4, k))
        return copies

    for k in range(chunks):
        for copy in bring_in(k):
            copy.start()
    for k in range(chunks):
        for copy in bring_in(k):
            copy.wait()
        bring(down_in, down, 3, k).start()
        upstream = g[:, part(k)]
        if has_other:
            upstream = jnp.where(which[1] == 1, other[:, part(k)], upstream)
            g[:, part(k)] = upstream
        gp = (upstream.astype(F32) * e[:, part(k)].astype(F32)).astype(BF)
        term = dot(gp, up[:, part(k)], ((1,), (1,)))
        if k == 0:
            acc[...] = term
        else:
            acc[...] += term
    h[...] = acc[...].astype(BF)
    keep = pltpu.make_async_copy(h, h_out, out_sems.at[chunks])
    keep.start()
    for k in range(chunks):
        bring(down_in, down, 3, k).wait()
        total = g[:, part(k)].astype(F32) + dot(h[...], down[:, part(k)], ((1,), (0,)))
        out[:, part(k)] = total.astype(BF)
        pltpu.make_async_copy(out.at[:, part(k)], passed.at[:, part(k)], out_sems.at[k]).start()
    for k in range(chunks):
        pltpu.make_async_copy(out.at[:, part(k)], passed.at[:, part(k)], out_sems.at[k]).wait()
    keep.wait()


def one_turn(which, g, embedded, up, down, other=None, chunks=4):
    rows, width = g.shape
    rank = up.shape[0]
    operands = [g, embedded, up, down] + ([] if other is None else [other])
    anywhere = pl.BlockSpec(memory_space=pl.ANY)
    return pl.pallas_call(
        functools.partial(turn_kernel, chunks, other is not None),
        out_shape=(jax.ShapeDtypeStruct((rows, width), BF), jax.ShapeDtypeStruct((rows, rank), BF)),
        in_specs=[pl.BlockSpec(memory_space=pltpu.SMEM)] + [anywhere] * len(operands),
        out_specs=(anywhere, anywhere),
        scratch_shapes=[
            pltpu.VMEM((rows, width), BF),
            pltpu.VMEM((rows, width), BF),
            pltpu.VMEM((rank, width), BF),
            pltpu.VMEM((rank, width), BF),
            pltpu.VMEM((rows, width), BF),
            pltpu.VMEM((rows, width), BF),
            pltpu.VMEM((rows, rank), BF),
            pltpu.VMEM((rows, rank), F32),
            pltpu.SemaphoreType.DMA((5, chunks)),
            pltpu.SemaphoreType.DMA((chunks + 1,)),
        ],
        compiler_params=pltpu.CompilerParams(vmem_limit_bytes=24 << 20),
        cost_estimate=pl.CostEstimate(
            flops=4 * rows * width * rank, bytes_accessed=4 * rank * width + 6 * rows * width, transcendentals=0
        ),
    )(which, *operands)


def ring(sizes, place, shift):
    pairs = []
    stride = 1
    for size in sizes[place + 1 :]:
        stride *= size
    count = 1
    for size in sizes:
        count *= size
    for i in range(count):
        here = i // stride % sizes[place]
        pairs.append((i, i + ((here + shift) % sizes[place] - here) * stride))
    return pairs


def sum_over_section(terms, sections, section_id):
    chips = sections // 2
    chip, core = section_id // 2, section_id % 2
    pieces, rows, width = terms.shape
    terms = terms.reshape(pieces, chips, 2, rows // sections, width)
    other = lax.dynamic_index_in_dim(terms, 1 - core, 2, keepdims=False)
    mine = lax.dynamic_index_in_dim(terms, core, 2, keepdims=False)
    other = lax.ppermute(other, "section", ring((chips, 2), 1, 1))
    both = (mine.astype(F32) + other.astype(F32)).astype(BF)
    total = lax.dynamic_index_in_dim(both, chip, 1, keepdims=False).astype(F32)
    for d in range(1, chips):
        block = lax.dynamic_index_in_dim(both, (chip + d) % chips, 1, keepdims=False)
        total = total + lax.ppermute(block, "section", ring((chips, 2), 0, d)).astype(F32)
    return total.astype(BF).reshape(-1, width)


def local(embedded, saved_inputs, cotangent, w_down, w_up, bias, owners, row_ids):
    sections = lax.axis_size("section")
    replicas = lax.axis_size("dp")
    section_id = lax.axis_index("section")
    devices = sections * replicas
    pieces, rows, width = embedded.shape
    features = width // E
    rank = w_down.shape[1]
    share = rows // sections
    turns = sections + pieces - 1
    down, up = w_down[0], w_up[0]

    held_g, held_h = [None] * pieces, [None] * pieces
    odd = (sections - 1 - section_id) % 2 == 1
    layer_in = saved_inputs[0].reshape(-1, width)

    def piece_of(held, k):
        return jnp.where(odd, held[1 - k], held[k])

    def terms_of(k, passed):
        g = piece_of(held_g, k).astype(F32)
        bottom = jnp.where(section_id == 0, passed, jnp.zeros((), BF)).astype(F32)
        term = (g * product[k] + bottom).astype(BF)
        return term, in_columns((g * embedded[k].astype(F32)).astype(BF), replicas)

    for turn in range(turns):
        piece = turn - (sections - 1 - section_id)
        valid = (piece >= 0) & (piece < pieces)
        clipped = jnp.clip(piece, 0, pieces - 1)
        if turn == 2:
            incoming, latent = after(incoming, latent)
        if turn == 4:
            incoming, product = after(incoming, product)
        if turn == 6:
            incoming, all_in, put, ids = after(incoming, all_in, put, ids)
        top = section_id == sections - 1
        which = jnp.stack([clipped, top.astype(jnp.int32)])
        if turn == 0:
            incoming = cotangent[0]
            passed, h = one_turn(which, incoming, embedded, up, down)
        elif turn < pieces:
            passed, h = one_turn(which, incoming, embedded, up, down, cotangent[turn])
            incoming = jnp.where(top, cotangent[turn], after(incoming, passed)[0])
        else:
            passed, h = one_turn(which, incoming, embedded, up, down)
        if turn < turns - 1:
            pairs = [(s, s - 1) for s in range(1, sections) if 0 <= turn - (sections - 1 - s) < pieces]
            arriving = lax.ppermute(passed, "section", pairs)
        slot = turn % pieces
        if turn < pieces:
            held_g[slot], held_h[slot] = incoming, h
        else:
            old_g, old_h, _ = after(held_g[slot], held_h[slot], passed)
            held_g[slot] = jnp.where(valid, incoming, old_g)
            held_h[slot] = jnp.where(valid, h, old_h)

        if turn == 1:
            there = rows_major(after(layer_in, passed)[0])
            latent = dot(there, down, ((1,), (1,))).astype(BF)
            all_in = rows_major(exchange(rows_major(in_columns(there, replicas)), "dp"))
        if turn == 3:
            latent, _ = after(latent, passed)
            product = (dot(latent, up, ((1,), (0,))) + bias[0]).reshape(pieces, rows, width)
            all_latent = lax.all_gather(latent, "dp", axis=0)
        if turn == 5:
            own, ids, _ = after(owners, row_ids, passed)
            own = lax.dynamic_slice_in_dim(own, section_id * share, share, 0).transpose(2, 1, 0, 3).reshape(-1)
            ids = lax.dynamic_slice_in_dim(ids, section_id * share, share, 0).transpose(2, 1, 0).reshape(-1)
            order = jnp.arange(own.shape[0], dtype=jnp.int32)
            earlier = (own[:, None] == own[None, :]) & (order[:, None] < order[None, :])
            place = own * CAP + jnp.sum(earlier.astype(jnp.int32), axis=0)
            put = jnp.arange(devices * CAP, dtype=jnp.int32)[:, None] == place[None, :]
            send_ids = jnp.sum(jnp.where(put, ids[None, :], 0), axis=1)
            put = put.astype(BF)
            ids = jnp.stack([send_ids // 256, send_ids % 256], axis=1).astype(BF)
            ids = rows_major(jnp.pad(ids, ((0, 0), (0, 126))))
        if turn == sections - 1:
            early = terms_of(0, passed)
        if turn == sections - 1:
            arriving, *early = after(arriving, *early)
        if turn < turns - 1:
            incoming = arriving
    terms, columns = zip(early, terms_of(1, passed))
    all_h = lax.all_gather(jnp.stack([piece_of(held_h, k) for k in range(pieces)]), "dp", axis=0)
    summed = sum_over_section(jnp.stack(terms), sections, section_id)
    all_gp = exchange(jnp.concatenate(columns, axis=1), "dp")

    row_grads = in_columns(summed, features).reshape(-1, E)
    send = rows_major(dot(put, row_grads, ((1,), (0,))).astype(BF))
    send = jnp.concatenate([send, ids], axis=1).reshape(devices, CAP, -1)
    send, all_gp, all_latent = after(send, all_gp, all_latent)
    got = exchange(send, ("section", "dp")).reshape(devices * CAP, -1)
    got = rows_major(got)

    all_in = all_in.reshape(replicas, pieces, rows, -1)
    grad_down = dot(all_h, all_in, ((0, 1, 2), (0, 1, 2)))
    grad_up = dot(all_latent, all_gp, ((0, 1), (0, 1)))
    grad_bias = jnp.sum(all_gp.astype(F32), axis=(0, 1))

    got_ids = (got[:, E].astype(F32) * 256 + got[:, E + 1].astype(F32)).astype(jnp.int32)
    table_put = (jnp.arange(ROWS_DEV, dtype=jnp.int32)[:, None] == got_ids[None, :]).astype(BF)
    table_grad = dot(table_put, got[:, :E], ((1,), (0,)))
    return (grad_down[None], grad_up[None], grad_bias[None], table_grad)


def solution(mesh):
    placed = (
        P(None, "dp", None),
        P("section", None, "dp", None),
        P(None, "dp", None),
        P("section", None, None),
        P("section", None, None),
        P("section", None),
        P("dp", None, None, None),
        P("dp", None, None),
    )
    return jax.shard_map(
        local,
        mesh=mesh,
        in_specs=placed,
        out_specs=(
            P("section", None, "dp"),
            P("section", None, "dp"),
            P("section", "dp"),
            P(("section", "dp"), None),
        ),
        check_vma=False,
    )
```

```python
import jax
import jax.numpy as jnp
from jax import lax
from jax.experimental.layout import Layout, with_layout_constraint
from jax.sharding import PartitionSpec as P

E = 256
ROWS_DEV = 2048
CAP = 8
BF = jnp.bfloat16
F32 = jnp.float32


def dot(a, b, dims):
    return lax.dot_general(a, b, (dims, ((), ())), preferred_element_type=F32)


def exchange(pieces, axis):
    return lax.all_to_all(pieces, axis, split_axis=0, concat_axis=0, tiled=True)


def rows_major(array):
    return with_layout_constraint(array, Layout(major_to_minor=tuple(range(array.ndim))))


def after(*arrays):
    return lax.optimization_barrier(arrays)


def in_columns(rows, devices):
    return rows.reshape(rows.shape[0], devices, -1).transpose(1, 0, 2)


def ring(sizes, place, shift):
    pairs = []
    stride = 1
    for size in sizes[place + 1 :]:
        stride *= size
    count = 1
    for size in sizes:
        count *= size
    for i in range(count):
        here = i // stride % sizes[place]
        pairs.append((i, i + ((here + shift) % sizes[place] - here) * stride))
    return pairs


def sum_over_section(terms, sections, section_id, later):
    chips = sections // 2
    chip, core = section_id // 2, section_id % 2
    pieces, rows, width = terms.shape
    terms = terms.reshape(pieces, chips, 2, rows // sections, width)
    other = lax.dynamic_index_in_dim(terms, 1 - core, 2, keepdims=False)
    mine = lax.dynamic_index_in_dim(terms, core, 2, keepdims=False)
    other = lax.ppermute(other, "section", ring((chips, 2), 1, 1))
    both = (mine.astype(F32) + other.astype(F32)).astype(BF)
    both, later = after(both, later)
    total = lax.dynamic_index_in_dim(both, chip, 1, keepdims=False).astype(F32)
    for d in range(1, chips):
        block = lax.dynamic_index_in_dim(both, (chip + d) % chips, 1, keepdims=False)
        total = total + lax.ppermute(block, "section", ring((chips, 2), 0, d)).astype(F32)
    return total.astype(BF).reshape(-1, width), later


def local(embedded, saved_inputs, cotangent, w_down, w_up, bias, owners, row_ids):
    sections = lax.axis_size("section")
    replicas = lax.axis_size("dp")
    section_id = lax.axis_index("section")
    devices = sections * replicas
    pieces, rows, width = embedded.shape
    features = width // E
    rank = w_down.shape[1]
    share = rows // sections
    turns = sections + pieces - 1
    down, up = w_down[0], w_up[0]

    held_g, held_h = [None] * pieces, [None] * pieces
    odd = (sections - 1 - section_id) % 2 == 1
    layer_in = saved_inputs[0].reshape(-1, width)

    def piece_of(held, k):
        return jnp.where(odd, held[1 - k], held[k])

    def terms_of(k, passed):
        g = piece_of(held_g, k).astype(F32)
        bottom = jnp.where(section_id == 0, passed, jnp.zeros((), BF)).astype(F32)
        term = (g * product[k] + bottom).astype(BF)
        return term, in_columns((g * embedded[k].astype(F32)).astype(BF), replicas)

    for turn in range(turns):
        piece = turn - (sections - 1 - section_id)
        valid = (piece >= 0) & (piece < pieces)
        clipped = jnp.clip(piece, 0, pieces - 1)
        first = lax.dynamic_index_in_dim(embedded, clipped, 0, keepdims=False)
        if turn == 2:
            incoming, latent = after(incoming, latent)
        if turn == 4:
            incoming, product = after(incoming, product)
        if turn == 6:
            incoming, all_in, put, ids = after(incoming, all_in, put, ids)
        if turn == 0:
            incoming = cotangent[0]
        elif turn < pieces:
            incoming = jnp.where(section_id == sections - 1, cotangent[turn], incoming)
        gp = (incoming.astype(F32) * first.astype(F32)).astype(BF)
        h = dot(gp, up, ((1,), (1,))).astype(BF)
        passed = (incoming.astype(F32) + dot(h, down, ((1,), (0,)))).astype(BF)
        if turn < turns - 1:
            pairs = [(s, s - 1) for s in range(1, sections) if 0 <= turn - (sections - 1 - s) < pieces]
            arriving = lax.ppermute(passed, "section", pairs)
        slot = turn % pieces
        if turn < pieces:
            held_g[slot], held_h[slot] = incoming, h
        else:
            old_g, old_h, _ = after(held_g[slot], held_h[slot], passed)
            held_g[slot] = jnp.where(valid, incoming, old_g)
            held_h[slot] = jnp.where(valid, h, old_h)

        if turn == 1:
            there = rows_major(after(layer_in, passed)[0])
            latent = dot(there, down, ((1,), (1,))).astype(BF)
            all_in = rows_major(exchange(rows_major(in_columns(there, replicas)), "dp"))
        if turn == 3:
            latent, _ = after(latent, passed)
            product = (dot(latent, up, ((1,), (0,))) + bias[0]).reshape(pieces, rows, width)
            all_latent = lax.all_gather(latent, "dp", axis=0)
        if turn == 5:
            own, ids, _ = after(owners, row_ids, passed)
            own = lax.dynamic_slice_in_dim(own, section_id * share, share, 0).transpose(2, 1, 0, 3).reshape(-1)
            ids = lax.dynamic_slice_in_dim(ids, section_id * share, share, 0).transpose(2, 1, 0).reshape(-1)
            order = jnp.arange(own.shape[0], dtype=jnp.int32)
            earlier = (own[:, None] == own[None, :]) & (order[:, None] < order[None, :])
            place = own * CAP + jnp.sum(earlier.astype(jnp.int32), axis=0)
            put = jnp.arange(devices * CAP, dtype=jnp.int32)[:, None] == place[None, :]
            send_ids = jnp.sum(jnp.where(put, ids[None, :], 0), axis=1)
            put = put.astype(BF)
            ids = jnp.stack([send_ids // 256, send_ids % 256], axis=1).astype(BF)
            ids = rows_major(jnp.pad(ids, ((0, 0), (0, 126))))
        if turn == sections - 1:
            early = terms_of(0, passed)
            arriving, *early = after(arriving, *early)
        if turn < turns - 1:
            incoming = arriving
    terms, columns = zip(early, terms_of(1, passed))
    all_h = lax.all_gather(jnp.stack([piece_of(held_h, k) for k in range(pieces)]), "dp", axis=0)
    columns = list(columns)
    summed, columns[0] = sum_over_section(jnp.stack(terms), sections, section_id, columns[0])
    all_gp = [exchange(columns[0], "dp")]

    row_grads = in_columns(summed, features).reshape(-1, E)
    send = rows_major(dot(put, row_grads, ((1,), (0,))).astype(BF))
    send = jnp.concatenate([send, ids], axis=1).reshape(devices, CAP, -1)
    send, all_gp[0], all_latent = after(send, all_gp[0], all_latent)
    got = exchange(send, ("section", "dp")).reshape(devices * CAP, -1)
    got = rows_major(got)
    columns[1], got, all_h = after(columns[1], got, all_h)
    all_gp.append(exchange(columns[1], "dp"))

    all_in = all_in.reshape(replicas, pieces, rows, -1)
    grad_down = dot(all_h, all_in, ((0, 1, 2), (0, 1, 2)))
    all_latent = all_latent.reshape(replicas, pieces, rows, -1)
    grad_up = sum(dot(all_latent[:, k], all_gp[k], ((0, 1), (0, 1))) for k in range(pieces))
    grad_bias = sum(jnp.sum(gp.astype(F32), axis=(0, 1)) for gp in all_gp)

    got_ids = (got[:, E].astype(F32) * 256 + got[:, E + 1].astype(F32)).astype(jnp.int32)
    table_put = (jnp.arange(ROWS_DEV, dtype=jnp.int32)[:, None] == got_ids[None, :]).astype(BF)
    table_grad = dot(table_put, got[:, :E], ((1,), (0,)))
    return (grad_down[None], grad_up[None], grad_bias[None], table_grad)


def solution(mesh):
    placed = (
        P(None, "dp", None),
        P("section", None, "dp", None),
        P(None, "dp", None),
        P("section", None, None),
        P("section", None, None),
        P("section", None),
        P("dp", None, None, None),
        P("dp", None, None),
    )
    return jax.shard_map(
        local,
        mesh=mesh,
        in_specs=placed,
        out_specs=(
            P("section", None, "dp"),
            P("section", None, "dp"),
            P("section", "dp"),
            P(("section", "dp"), None),
        ),
        check_vma=False,
    )
```

```python
import jax
import jax.numpy as jnp
from jax import lax
from jax.experimental.layout import Layout, with_layout_constraint
from jax.sharding import PartitionSpec as P

E = 256
ROWS_DEV = 2048
CAP = 8
BF = jnp.bfloat16
F32 = jnp.float32


def dot(a, b, dims):
    return lax.dot_general(a, b, (dims, ((), ())), preferred_element_type=F32)


def exchange(pieces, axis):
    return lax.all_to_all(pieces, axis, split_axis=0, concat_axis=0, tiled=True)


def rows_major(array):
    return with_layout_constraint(array, Layout(major_to_minor=tuple(range(array.ndim))))


def after(*arrays):
    return lax.optimization_barrier(arrays)


def in_columns(rows, devices):
    return rows.reshape(rows.shape[0], devices, -1).transpose(1, 0, 2)


def ring(sizes, place, shift):
    pairs = []
    stride = 1
    for size in sizes[place + 1 :]:
        stride *= size
    count = 1
    for size in sizes:
        count *= size
    for i in range(count):
        here = i // stride % sizes[place]
        pairs.append((i, i + ((here + shift) % sizes[place] - here) * stride))
    return pairs


def sum_over_section(terms, sections, section_id):
    chips = sections // 2
    chip, core = section_id // 2, section_id % 2
    pieces, rows, width = terms.shape
    terms = terms.reshape(pieces, chips, 2, rows // sections, width)
    other = lax.dynamic_index_in_dim(terms, 1 - core, 2, keepdims=False)
    mine = lax.dynamic_index_in_dim(terms, core, 2, keepdims=False)
    other = lax.ppermute(other, "section", ring((chips, 2), 1, 1))
    both = (mine.astype(F32) + other.astype(F32)).astype(BF)
    total = lax.dynamic_index_in_dim(both, chip, 1, keepdims=False).astype(F32)
    for d in range(1, chips):
        block = lax.dynamic_index_in_dim(both, (chip + d) % chips, 1, keepdims=False)
        total = total + lax.ppermute(block, "section", ring((chips, 2), 0, d)).astype(F32)
    return total.astype(BF).reshape(-1, width)


def local(embedded, saved_inputs, cotangent, w_down, w_up, bias, owners, row_ids):
    sections = lax.axis_size("section")
    replicas = lax.axis_size("dp")
    section_id = lax.axis_index("section")
    devices = sections * replicas
    pieces, rows, width = embedded.shape
    features = width // E
    rank = w_down.shape[1]
    share = rows // sections
    turns = sections + pieces - 1
    down, up = w_down[0], w_up[0]

    held_g, held_h = [None] * pieces, [None] * pieces
    odd = (sections - 1 - section_id) % 2 == 1
    layer_in = saved_inputs[0].reshape(-1, width)

    def piece_of(held, k):
        return jnp.where(odd, held[1 - k], held[k])

    def terms_of(k, passed):
        g = piece_of(held_g, k).astype(F32)
        bottom = jnp.where(section_id == 0, passed, jnp.zeros((), BF)).astype(F32)
        term = (g * product[k] + bottom).astype(BF)
        return term, in_columns((g * embedded[k].astype(F32)).astype(BF), replicas)

    for turn in range(turns):
        piece = turn - (sections - 1 - section_id)
        valid = (piece >= 0) & (piece < pieces)
        clipped = jnp.clip(piece, 0, pieces - 1)
        first = lax.dynamic_index_in_dim(embedded, clipped, 0, keepdims=False)
        if turn == 2:
            incoming, latent = after(incoming, latent)
        if turn == 4:
            incoming, product = after(incoming, product)
        if turn == 6:
            incoming, all_in, put, ids = after(incoming, all_in, put, ids)
        if turn == 0:
            incoming = cotangent[0]
        elif turn < pieces:
            incoming = jnp.where(section_id == sections - 1, cotangent[turn], incoming)
        gp = (incoming.astype(F32) * first.astype(F32)).astype(BF)
        h = dot(gp, up, ((1,), (1,))).astype(BF)
        passed = (incoming.astype(F32) + dot(h, down, ((1,), (0,)))).astype(BF)
        if turn < turns - 1:
            pairs = [(s, s - 1) for s in range(1, sections) if 0 <= turn - (sections - 1 - s) < pieces]
            arriving = lax.ppermute(passed, "section", pairs)
        slot = turn % pieces
        if turn < pieces:
            held_g[slot], held_h[slot] = incoming, h
        else:
            old_g, old_h, _ = after(held_g[slot], held_h[slot], passed)
            held_g[slot] = jnp.where(valid, incoming, old_g)
            held_h[slot] = jnp.where(valid, h, old_h)

        if turn == 1:
            there = rows_major(after(layer_in, passed)[0])
            latent = dot(there, down, ((1,), (1,))).astype(BF)
            all_in = rows_major(exchange(rows_major(in_columns(there, replicas)), "dp"))
        if turn == 3:
            latent, _ = after(latent, passed)
            product = (dot(latent, up, ((1,), (0,))) + bias[0]).reshape(pieces, rows, width)
            all_latent = lax.all_gather(latent, "dp", axis=0)
        if turn == 5:
            own, ids, _ = after(owners, row_ids, passed)
            own = lax.dynamic_slice_in_dim(own, section_id * share, share, 0).transpose(2, 1, 0, 3).reshape(-1)
            ids = lax.dynamic_slice_in_dim(ids, section_id * share, share, 0).transpose(2, 1, 0).reshape(-1)
            order = jnp.arange(own.shape[0], dtype=jnp.int32)
            earlier = (own[:, None] == own[None, :]) & (order[:, None] < order[None, :])
            place = own * CAP + jnp.sum(earlier.astype(jnp.int32), axis=0)
            put = jnp.arange(devices * CAP, dtype=jnp.int32)[:, None] == place[None, :]
            send_ids = jnp.sum(jnp.where(put, ids[None, :], 0), axis=1)
            put = put.astype(BF)
            ids = jnp.stack([send_ids // 256, send_ids % 256], axis=1).astype(BF)
            ids = rows_major(jnp.pad(ids, ((0, 0), (0, 126))))
        if turn == sections - 1:
            early = terms_of(0, passed)
            arriving, *early = after(arriving, *early)
        if turn < turns - 1:
            incoming = arriving
    terms, columns = zip(early, terms_of(1, passed))
    all_h = lax.all_gather(jnp.stack([piece_of(held_h, k) for k in range(pieces)]), "dp", axis=0)
    summed = sum_over_section(jnp.stack(terms), sections, section_id)
    all_gp = exchange(jnp.concatenate(columns, axis=1), "dp")

    row_grads = in_columns(summed, features).reshape(-1, E)
    send = rows_major(dot(put, row_grads, ((1,), (0,))).astype(BF))
    send = jnp.concatenate([send, ids], axis=1).reshape(devices, CAP, -1)
    send, all_gp, all_latent = after(send, all_gp, all_latent)
    got = exchange(send, ("section", "dp")).reshape(devices * CAP, -1)

    all_in = all_in.reshape(replicas, pieces, rows, -1)
    grad_up = dot(all_latent.reshape(replicas, -1, rank), all_gp, ((0, 1), (0, 1)))
    grad_bias = jnp.sum(all_gp.astype(F32), axis=(0, 1))
    grad_down = dot(all_h, all_in, ((0, 1, 2), (0, 1, 2)))
    got, grad_down = after(got, grad_down)
    got = rows_major(got)

    got_ids = (got[:, E].astype(F32) * 256 + got[:, E + 1].astype(F32)).astype(jnp.int32)
    table_put = (jnp.arange(ROWS_DEV, dtype=jnp.int32)[:, None] == got_ids[None, :]).astype(BF)
    table_grad = dot(table_put, got[:, :E], ((1,), (0,)))
    return (grad_down[None], grad_up[None], grad_bias[None], table_grad)


def solution(mesh):
    placed = (
        P(None, "dp", None),
        P("section", None, "dp", None),
        P(None, "dp", None),
        P("section", None, None),
        P("section", None, None),
        P("section", None),
        P("dp", None, None, None),
        P("dp", None, None),
    )
    return jax.shard_map(
        local,
        mesh=mesh,
        in_specs=placed,
        out_specs=(
            P("section", None, "dp"),
            P("section", None, "dp"),
            P("section", "dp"),
            P(("section", "dp"), None),
        ),
        check_vma=False,
    )
```

```python
import jax
import jax.numpy as jnp
from jax import lax
from jax.experimental.layout import Layout, with_layout_constraint
from jax.sharding import PartitionSpec as P

E = 256
ROWS_DEV = 2048
CAP = 8
BF = jnp.bfloat16
F32 = jnp.float32


def dot(a, b, dims):
    return lax.dot_general(a, b, (dims, ((), ())), preferred_element_type=F32)


def exchange(pieces, axis):
    return lax.all_to_all(pieces, axis, split_axis=0, concat_axis=0, tiled=True)


def rows_major(array):
    return with_layout_constraint(array, Layout(major_to_minor=tuple(range(array.ndim))))


def after(*arrays):
    return lax.optimization_barrier(arrays)


def in_columns(rows, devices):
    return rows.reshape(rows.shape[0], devices, -1).transpose(1, 0, 2)


def ring(sizes, place, shift):
    pairs = []
    stride = 1
    for size in sizes[place + 1 :]:
        stride *= size
    count = 1
    for size in sizes:
        count *= size
    for i in range(count):
        here = i // stride % sizes[place]
        pairs.append((i, i + ((here + shift) % sizes[place] - here) * stride))
    return pairs


def sum_over_section(terms, sections, section_id):
    chips = sections // 2
    chip, core = section_id // 2, section_id % 2
    pieces, rows, width = terms.shape
    terms = terms.reshape(pieces, chips, 2, rows // sections, width)
    other = lax.dynamic_index_in_dim(terms, 1 - core, 2, keepdims=False)
    mine = lax.dynamic_index_in_dim(terms, core, 2, keepdims=False)
    other = lax.ppermute(other, "section", ring((chips, 2), 1, 1))
    both = (mine.astype(F32) + other.astype(F32)).astype(BF)
    total = lax.dynamic_index_in_dim(both, chip, 1, keepdims=False).astype(F32)
    for d in range(1, chips):
        block = lax.dynamic_index_in_dim(both, (chip + d) % chips, 1, keepdims=False)
        total = total + lax.ppermute(block, "section", ring((chips, 2), 0, d)).astype(F32)
    return total.astype(BF).reshape(-1, width)


def local(embedded, saved_inputs, cotangent, w_down, w_up, bias, owners, row_ids):
    sections = lax.axis_size("section")
    replicas = lax.axis_size("dp")
    section_id = lax.axis_index("section")
    devices = sections * replicas
    pieces, rows, width = embedded.shape
    features = width // E
    rank = w_down.shape[1]
    share = rows // sections
    turns = sections + pieces - 1
    down, up = w_down[0], w_up[0]

    held_g, held_h = [None] * pieces, [None] * pieces
    odd = (sections - 1 - section_id) % 2 == 1
    layer_in = saved_inputs[0].reshape(-1, width)

    def piece_of(held, k):
        return jnp.where(odd, held[1 - k], held[k])

    def terms_of(k, passed):
        g = piece_of(held_g, k).astype(F32)
        bottom = jnp.where(section_id == 0, passed, jnp.zeros((), BF)).astype(F32)
        term = (g * product[k] + bottom).astype(BF)
        return term, in_columns((g * embedded[k].astype(F32)).astype(BF), replicas)

    for turn in range(turns):
        piece = turn - (sections - 1 - section_id)
        valid = (piece >= 0) & (piece < pieces)
        clipped = jnp.clip(piece, 0, pieces - 1)
        first = lax.dynamic_index_in_dim(embedded, clipped, 0, keepdims=False)
        if turn == 2:
            incoming, latent = after(incoming, latent)
        if turn == sections:
            incoming, early_gp = after(incoming, early_gp)
        if turn == 4:
            incoming, product = after(incoming, product)
        if turn == 6:
            incoming, all_in, put, ids = after(incoming, all_in, put, ids)
        if turn == 0:
            incoming = cotangent[0]
        elif turn < pieces:
            incoming = jnp.where(section_id == sections - 1, cotangent[turn], incoming)
        gp = (incoming.astype(F32) * first.astype(F32)).astype(BF)
        h = dot(gp, up, ((1,), (1,))).astype(BF)
        passed = (incoming.astype(F32) + dot(h, down, ((1,), (0,)))).astype(BF)
        if turn < turns - 1:
            pairs = [(s, s - 1) for s in range(1, sections) if 0 <= turn - (sections - 1 - s) < pieces]
            arriving = lax.ppermute(passed, "section", pairs)
        slot = turn % pieces
        if turn < pieces:
            held_g[slot], held_h[slot] = incoming, h
        else:
            old_g, old_h, _ = after(held_g[slot], held_h[slot], passed)
            held_g[slot] = jnp.where(valid, incoming, old_g)
            held_h[slot] = jnp.where(valid, h, old_h)

        if turn == 1:
            there = rows_major(after(layer_in, passed)[0])
            latent = dot(there, down, ((1,), (1,))).astype(BF)
            all_in = rows_major(exchange(rows_major(in_columns(there, replicas)), "dp"))
        if turn == 3:
            latent, _ = after(latent, passed)
            product = (dot(latent, up, ((1,), (0,))) + bias[0]).reshape(pieces, rows, width)
            all_latent = lax.all_gather(latent, "dp", axis=0)
        if turn == 5:
            own, ids, _ = after(owners, row_ids, passed)
            own = lax.dynamic_slice_in_dim(own, section_id * share, share, 0).transpose(2, 1, 0, 3).reshape(-1)
            ids = lax.dynamic_slice_in_dim(ids, section_id * share, share, 0).transpose(2, 1, 0).reshape(-1)
            order = jnp.arange(own.shape[0], dtype=jnp.int32)
            earlier = (own[:, None] == own[None, :]) & (order[:, None] < order[None, :])
            place = own * CAP + jnp.sum(earlier.astype(jnp.int32), axis=0)
            put = jnp.arange(devices * CAP, dtype=jnp.int32)[:, None] == place[None, :]
            send_ids = jnp.sum(jnp.where(put, ids[None, :], 0), axis=1)
            put = put.astype(BF)
            ids = jnp.stack([send_ids // 256, send_ids % 256], axis=1).astype(BF)
            ids = rows_major(jnp.pad(ids, ((0, 0), (0, 126))))
        if turn == sections - 1:
            early = terms_of(0, passed)
            arriving, *early = after(arriving, *early)
            early_gp = exchange(early[1], "dp")
        if turn < turns - 1:
            incoming = arriving
    terms, columns = zip(early, terms_of(1, passed))
    all_h = lax.all_gather(jnp.stack([piece_of(held_h, k) for k in range(pieces)]), "dp", axis=0)
    summed = sum_over_section(jnp.stack(terms), sections, section_id)
    late, early_gp = after(columns[1], early_gp)
    all_gp = [early_gp, exchange(late, "dp")]

    row_grads = in_columns(summed, features).reshape(-1, E)
    send = rows_major(dot(put, row_grads, ((1,), (0,))).astype(BF))
    send = jnp.concatenate([send, ids], axis=1).reshape(devices, CAP, -1)
    send, all_gp[1], all_latent = after(send, all_gp[1], all_latent)
    got = exchange(send, ("section", "dp")).reshape(devices * CAP, -1)

    all_in = all_in.reshape(replicas, pieces, rows, -1)
    all_latent = all_latent.reshape(replicas, pieces, rows, rank)
    grad_up = sum(dot(all_latent[:, k], all_gp[k], ((0, 1), (0, 1))) for k in range(pieces))
    grad_bias = sum(jnp.sum(gp.astype(F32), axis=(0, 1)) for gp in all_gp)
    grad_down = dot(all_h, all_in, ((0, 1, 2), (0, 1, 2)))
    got, grad_down = after(got, grad_down)
    got = rows_major(got)

    got_ids = (got[:, E].astype(F32) * 256 + got[:, E + 1].astype(F32)).astype(jnp.int32)
    table_put = (jnp.arange(ROWS_DEV, dtype=jnp.int32)[:, None] == got_ids[None, :]).astype(BF)
    table_grad = dot(table_put, got[:, :E], ((1,), (0,)))
    return (grad_down[None], grad_up[None], grad_bias[None], table_grad)


def solution(mesh):
    placed = (
        P(None, "dp", None),
        P("section", None, "dp", None),
        P(None, "dp", None),
        P("section", None, None),
        P("section", None, None),
        P("section", None),
        P("dp", None, None, None),
        P("dp", None, None),
    )
    return jax.shard_map(
        local,
        mesh=mesh,
        in_specs=placed,
        out_specs=(
            P("section", None, "dp"),
            P("section", None, "dp"),
            P("section", "dp"),
            P(("section", "dp"), None),
        ),
        check_vma=False,
    )
```

```python
import jax
import jax.numpy as jnp
from jax import lax
from jax.experimental.layout import Layout, with_layout_constraint
from jax.sharding import PartitionSpec as P

E = 256
ROWS_DEV = 2048
CAP = 8
BF = jnp.bfloat16
F32 = jnp.float32


def dot(a, b, dims):
    return lax.dot_general(a, b, (dims, ((), ())), preferred_element_type=F32)


def exchange(pieces, axis):
    return lax.all_to_all(pieces, axis, split_axis=0, concat_axis=0, tiled=True)


def rows_major(array):
    return with_layout_constraint(array, Layout(major_to_minor=tuple(range(array.ndim))))


def after(*arrays):
    return lax.optimization_barrier(arrays)


def in_columns(rows, devices):
    return rows.reshape(rows.shape[0], devices, -1).transpose(1, 0, 2)


def ring(sizes, place, shift):
    pairs = []
    stride = 1
    for size in sizes[place + 1 :]:
        stride *= size
    count = 1
    for size in sizes:
        count *= size
    for i in range(count):
        here = i // stride % sizes[place]
        pairs.append((i, i + ((here + shift) % sizes[place] - here) * stride))
    return pairs


def sum_over_section(terms, sections, section_id):
    chips = sections // 2
    chip, core = section_id // 2, section_id % 2
    pieces, rows, width = terms.shape
    terms = terms.reshape(pieces, chips, 2, rows // sections, width)
    other = lax.dynamic_index_in_dim(terms, 1 - core, 2, keepdims=False)
    mine = lax.dynamic_index_in_dim(terms, core, 2, keepdims=False)
    other = lax.ppermute(other, "section", ring((chips, 2), 1, 1))
    both = (mine.astype(F32) + other.astype(F32)).astype(BF)
    total = lax.dynamic_index_in_dim(both, chip, 1, keepdims=False).astype(F32)
    for d in range(1, chips):
        block = lax.dynamic_index_in_dim(both, (chip + d) % chips, 1, keepdims=False)
        total = total + lax.ppermute(block, "section", ring((chips, 2), 0, d)).astype(F32)
    return total.astype(BF).reshape(-1, width)


def local(embedded, saved_inputs, cotangent, w_down, w_up, bias, owners, row_ids):
    sections = lax.axis_size("section")
    replicas = lax.axis_size("dp")
    section_id = lax.axis_index("section")
    devices = sections * replicas
    pieces, rows, width = embedded.shape
    features = width // E
    rank = w_down.shape[1]
    share = rows // sections
    turns = sections + pieces - 1
    down, up = w_down[0], w_up[0]

    held_g, held_h = [None] * pieces, [None] * pieces
    odd = (sections - 1 - section_id) % 2 == 1
    layer_in = saved_inputs[0].reshape(-1, width)

    def piece_of(held, k):
        return jnp.where(odd, held[1 - k], held[k])

    def terms_of(k, passed):
        g = piece_of(held_g, k).astype(F32)
        bottom = jnp.where(section_id == 0, passed, jnp.zeros((), BF)).astype(F32)
        term = (g * product[k] + bottom).astype(BF)
        return term, in_columns((g * embedded[k].astype(F32)).astype(BF), replicas)

    for turn in range(turns):
        piece = turn - (sections - 1 - section_id)
        valid = (piece >= 0) & (piece < pieces)
        clipped = jnp.clip(piece, 0, pieces - 1)
        first = lax.dynamic_index_in_dim(embedded, clipped, 0, keepdims=False)
        if turn == 4:
            incoming, product = after(incoming, product)
        if turn == 6:
            incoming, all_in, put, ids = after(incoming, all_in, put, ids)
        if turn == 0:
            incoming = cotangent[0]
        elif turn < pieces:
            again, top = after(incoming, cotangent[turn])
            g = jnp.where(section_id == sections - 1, cotangent[turn], incoming)
            incoming = jnp.where(section_id == sections - 1, top, again)
        if turn == 0 or turn >= pieces:
            g = incoming
        gp = (g.astype(F32) * first.astype(F32)).astype(BF)
        h = dot(gp, up, ((1,), (1,))).astype(BF)
        passed = (incoming.astype(F32) + dot(h, down, ((1,), (0,)))).astype(BF)
        if turn < turns - 1:
            pairs = [(s, s - 1) for s in range(1, sections) if 0 <= turn - (sections - 1 - s) < pieces]
            arriving = lax.ppermute(passed, "section", pairs)
        slot = turn % pieces
        if turn < pieces:
            held_g[slot], held_h[slot] = incoming, h
        else:
            old_g, old_h, _ = after(held_g[slot], held_h[slot], passed)
            held_g[slot] = jnp.where(valid, incoming, old_g)
            held_h[slot] = jnp.where(valid, h, old_h)

        if turn == 1:
            there = rows_major(after(layer_in, passed)[0])
            all_in = rows_major(exchange(rows_major(in_columns(there, replicas)), "dp"))
        if turn == 3:
            there, _ = after(layer_in, passed)
            latent = dot(there, down, ((1,), (1,))).astype(BF)
            product = (dot(latent, up, ((1,), (0,))) + bias[0]).reshape(pieces, rows, width)
            all_latent = lax.all_gather(latent, "dp", axis=0)
        if turn == 5:
            own, ids, _ = after(owners, row_ids, passed)
            own = lax.dynamic_slice_in_dim(own, section_id * share, share, 0).transpose(2, 1, 0, 3).reshape(-1)
            ids = lax.dynamic_slice_in_dim(ids, section_id * share, share, 0).transpose(2, 1, 0).reshape(-1)
            order = jnp.arange(own.shape[0], dtype=jnp.int32)
            earlier = (own[:, None] == own[None, :]) & (order[:, None] < order[None, :])
            place = own * CAP + jnp.sum(earlier.astype(jnp.int32), axis=0)
            put = jnp.arange(devices * CAP, dtype=jnp.int32)[:, None] == place[None, :]
            send_ids = jnp.sum(jnp.where(put, ids[None, :], 0), axis=1)
            put = put.astype(BF)
            ids = jnp.stack([send_ids // 256, send_ids % 256], axis=1).astype(BF)
            ids = rows_major(jnp.pad(ids, ((0, 0), (0, 126))))
        if turn == sections - 1:
            early = terms_of(0, passed)
            arriving, *early = after(arriving, *early)
        if turn < turns - 1:
            incoming = arriving
    terms, columns = zip(early, terms_of(1, passed))
    all_h = lax.all_gather(jnp.stack([piece_of(held_h, k) for k in range(pieces)]), "dp", axis=0)
    summed = sum_over_section(jnp.stack(terms), sections, section_id)
    all_gp = exchange(jnp.concatenate(columns, axis=1), "dp")

    row_grads = in_columns(summed, features).reshape(-1, E)
    send = rows_major(dot(put, row_grads, ((1,), (0,))).astype(BF))
    send = jnp.concatenate([send, ids], axis=1).reshape(devices, CAP, -1)
    send, all_gp, all_latent = after(send, all_gp, all_latent)
    got = exchange(send, ("section", "dp")).reshape(devices * CAP, -1)

    all_in = all_in.reshape(replicas, pieces, rows, -1)
    grad_up = dot(all_latent.reshape(replicas, -1, rank), all_gp, ((0, 1), (0, 1)))
    grad_bias = jnp.sum(all_gp.astype(F32), axis=(0, 1))
    grad_down = dot(all_h, all_in, ((0, 1, 2), (0, 1, 2)))
    got, grad_down = after(got, grad_down)
    got = rows_major(got)

    got_ids = (got[:, E].astype(F32) * 256 + got[:, E + 1].astype(F32)).astype(jnp.int32)
    table_put = (jnp.arange(ROWS_DEV, dtype=jnp.int32)[:, None] == got_ids[None, :]).astype(BF)
    table_grad = dot(table_put, got[:, :E], ((1,), (0,)))
    return (grad_down[None], grad_up[None], grad_bias[None], table_grad)


def solution(mesh):
    placed = (
        P(None, "dp", None),
        P("section", None, "dp", None),
        P(None, "dp", None),
        P("section", None, None),
        P("section", None, None),
        P("section", None),
        P("dp", None, None, None),
        P("dp", None, None),
    )
    return jax.shard_map(
        local,
        mesh=mesh,
        in_specs=placed,
        out_specs=(
            P("section", None, "dp"),
            P("section", None, "dp"),
            P("section", "dp"),
            P(("section", "dp"), None),
        ),
        check_vma=False,
    )
```

```python
import jax
import jax.numpy as jnp
from jax import lax
from jax.experimental.layout import Layout, with_layout_constraint
from jax.sharding import PartitionSpec as P

E = 256
ROWS_DEV = 2048
CAP = 8
BF = jnp.bfloat16
F32 = jnp.float32


def dot(a, b, dims):
    return lax.dot_general(a, b, (dims, ((), ())), preferred_element_type=F32)


def exchange(pieces, axis):
    return lax.all_to_all(pieces, axis, split_axis=0, concat_axis=0, tiled=True)


def rows_major(array):
    return with_layout_constraint(array, Layout(major_to_minor=tuple(range(array.ndim))))


def after(*arrays):
    return lax.optimization_barrier(arrays)


def in_columns(rows, devices):
    return rows.reshape(rows.shape[0], devices, -1).transpose(1, 0, 2)


def ring(sizes, place, shift):
    pairs = []
    stride = 1
    for size in sizes[place + 1 :]:
        stride *= size
    count = 1
    for size in sizes:
        count *= size
    for i in range(count):
        here = i // stride % sizes[place]
        pairs.append((i, i + ((here + shift) % sizes[place] - here) * stride))
    return pairs


def sum_over_section(terms, sections, section_id):
    chips = sections // 2
    chip, core = section_id // 2, section_id % 2
    pieces, rows, width = terms.shape
    terms = terms.reshape(pieces, chips, 2, rows // sections, width)
    other = lax.dynamic_index_in_dim(terms, 1 - core, 2, keepdims=False)
    mine = lax.dynamic_index_in_dim(terms, core, 2, keepdims=False)
    other = lax.ppermute(other, "section", ring((chips, 2), 1, 1))
    both = (mine.astype(F32) + other.astype(F32)).astype(BF)
    total = lax.dynamic_index_in_dim(both, chip, 1, keepdims=False).astype(F32)
    for d in range(1, chips):
        block = lax.dynamic_index_in_dim(both, (chip + d) % chips, 1, keepdims=False)
        total = total + lax.ppermute(block, "section", ring((chips, 2), 0, d)).astype(F32)
    return total.astype(BF).reshape(-1, width)


def local(embedded, saved_inputs, cotangent, w_down, w_up, bias, owners, row_ids):
    sections = lax.axis_size("section")
    replicas = lax.axis_size("dp")
    section_id = lax.axis_index("section")
    devices = sections * replicas
    pieces, rows, width = embedded.shape
    features = width // E
    rank = w_down.shape[1]
    share = rows // sections
    turns = sections + pieces - 1
    down, up = w_down[0], w_up[0]

    held_g, held_h = [None] * pieces, [None] * pieces
    odd = (sections - 1 - section_id) % 2 == 1
    layer_in = saved_inputs[0].reshape(-1, width)

    def piece_of(held, k):
        return jnp.where(odd, held[1 - k], held[k])

    def terms_of(k, passed):
        g = piece_of(held_g, k).astype(F32)
        bottom = jnp.where(section_id == 0, passed, jnp.zeros((), BF)).astype(F32)
        term = (g * product[k] + bottom).astype(BF)
        return term, (g * embedded[k].astype(F32)).astype(BF)

    for turn in range(turns):
        piece = turn - (sections - 1 - section_id)
        valid = (piece >= 0) & (piece < pieces)
        clipped = jnp.clip(piece, 0, pieces - 1)
        first = lax.dynamic_index_in_dim(embedded, clipped, 0, keepdims=False)
        if turn == 4:
            incoming, product = after(incoming, product)
        if turn == 6:
            incoming, all_in, put, ids = after(incoming, all_in, put, ids)
        if turn == 0:
            incoming = cotangent[0]
        elif turn < pieces:
            again, top = after(incoming, cotangent[turn])
            g = jnp.where(section_id == sections - 1, cotangent[turn], incoming)
            incoming = jnp.where(section_id == sections - 1, top, again)
        if turn == 0 or turn >= pieces:
            g = incoming
        gp = (g.astype(F32) * first.astype(F32)).astype(BF)
        h = dot(gp, up, ((1,), (1,))).astype(BF)
        passed = (incoming.astype(F32) + dot(h, down, ((1,), (0,)))).astype(BF)
        if turn < turns - 1:
            pairs = [(s, s - 1) for s in range(1, sections) if 0 <= turn - (sections - 1 - s) < pieces]
            arriving = lax.ppermute(passed, "section", pairs)
        slot = turn % pieces
        if turn < pieces:
            held_g[slot], held_h[slot] = incoming, h
        else:
            old_g, old_h, _ = after(held_g[slot], held_h[slot], passed)
            held_g[slot] = jnp.where(valid, incoming, old_g)
            held_h[slot] = jnp.where(valid, h, old_h)

        if turn == 1:
            there = rows_major(after(layer_in, passed)[0])
            all_in = rows_major(exchange(rows_major(in_columns(there, replicas)), "dp"))
        if turn == 3:
            there, _ = after(layer_in, passed)
            latent = dot(there, down, ((1,), (1,))).astype(BF)
            product = (dot(latent, up, ((1,), (0,))) + bias[0]).reshape(pieces, rows, width)
            all_latent = lax.all_gather(latent, "dp", axis=0)
        if turn == 5:
            own, ids, _ = after(owners, row_ids, passed)
            own = lax.dynamic_slice_in_dim(own, section_id * share, share, 0).transpose(2, 1, 0, 3).reshape(-1)
            ids = lax.dynamic_slice_in_dim(ids, section_id * share, share, 0).transpose(2, 1, 0).reshape(-1)
            order = jnp.arange(own.shape[0], dtype=jnp.int32)
            earlier = (own[:, None] == own[None, :]) & (order[:, None] < order[None, :])
            place = own * CAP + jnp.sum(earlier.astype(jnp.int32), axis=0)
            put = jnp.arange(devices * CAP, dtype=jnp.int32)[:, None] == place[None, :]
            send_ids = jnp.sum(jnp.where(put, ids[None, :], 0), axis=1)
            put = put.astype(BF)
            ids = jnp.stack([send_ids // 256, send_ids % 256], axis=1).astype(BF)
            ids = rows_major(jnp.pad(ids, ((0, 0), (0, 126))))
        if turn == sections - 1:
            early = terms_of(0, passed)
            arriving, *early = after(arriving, *early)
        if turn < turns - 1:
            incoming = arriving
    terms, rows_of = zip(early, terms_of(1, passed))
    all_h = lax.all_gather(jnp.stack([piece_of(held_h, k) for k in range(pieces)]), "dp", axis=0)
    summed = sum_over_section(jnp.stack(terms), sections, section_id)
    all_gp = exchange(in_columns(jnp.concatenate(rows_of, axis=0), replicas), "dp")

    row_grads = in_columns(summed, features).reshape(-1, E)
    send = rows_major(dot(put, row_grads, ((1,), (0,))).astype(BF))
    send = jnp.concatenate([send, ids], axis=1).reshape(devices, CAP, -1)
    send, all_gp, all_latent = after(send, all_gp, all_latent)
    got = exchange(send, ("section", "dp")).reshape(devices * CAP, -1)

    all_in = all_in.reshape(replicas, pieces, rows, -1)
    grad_up = dot(all_latent.reshape(replicas, -1, rank), all_gp, ((0, 1), (0, 1)))
    grad_bias = jnp.sum(all_gp.astype(F32), axis=(0, 1))
    grad_down = dot(all_h, all_in, ((0, 1, 2), (0, 1, 2)))
    got, grad_down = after(got, grad_down)
    got = rows_major(got)

    got_ids = (got[:, E].astype(F32) * 256 + got[:, E + 1].astype(F32)).astype(jnp.int32)
    table_put = (jnp.arange(ROWS_DEV, dtype=jnp.int32)[:, None] == got_ids[None, :]).astype(BF)
    table_grad = dot(table_put, got[:, :E], ((1,), (0,)))
    return (grad_down[None], grad_up[None], grad_bias[None], table_grad)


def solution(mesh):
    placed = (
        P(None, "dp", None),
        P("section", None, "dp", None),
        P(None, "dp", None),
        P("section", None, None),
        P("section", None, None),
        P("section", None),
        P("dp", None, None, None),
        P("dp", None, None),
    )
    return jax.shard_map(
        local,
        mesh=mesh,
        in_specs=placed,
        out_specs=(
            P("section", None, "dp"),
            P("section", None, "dp"),
            P("section", "dp"),
            P(("section", "dp"), None),
        ),
        check_vma=False,
    )
```
